32 devices in a mesh: dp: 4 (over y, x), seq: 8 (over z, core).
Axes of the slice: x: 2, y: 2, z: 4, core: 2. Of those that a mesh axis runs over, the one named last changes fastest.
Arguments:
- block_in: bfloat16 [4, 4, 2048, 512], P('dp', None, 'seq'), may hold values from -6 to 6
- cotangent: bfloat16 [4, 4, 2048, 512], P('dp', None, 'seq'), may hold values from -6 to 6
- bucket_id: int32 [4, 4, 16], P('dp'), may hold values from 0 to 2, as said below
- assignment: int32 [4, 4], P('dp'), may hold values from 0 to 3, each once within a row
- norm_gain: float32 [512], replicated, may hold values from 0.25 to 1.75
- b_proj: bfloat16 [512, 512], replicated, may hold values from -0.25 to 0.25
- gamma_log: float32 [256], replicated, may hold values from -7 to -0.8
- nu_log: float32 [256], replicated
- theta_log: float32 [256], replicated, may hold values from -6.9 to 1.1
- c_proj: bfloat16 [512, 512], replicated, may hold values from -0.375 to 0.375
- d_skip: float32 [512], replicated, may hold values from -4 to 4
- glu_weight: bfloat16 [512, 1024], replicated, may hold values from -0.25 to 0.25
Outputs:
- block_out: bfloat16 [4, 4, 2048, 512], P('dp', None, 'seq')
- grad_in: bfloat16 [4, 4, 2048, 512], P('dp', None, 'seq')
- grad_norm_gain: float32 [512], replicated
- grad_b_proj: float32 [512, 512], replicated
- grad_gamma_log: float32 [256], replicated
- grad_nu_log: float32 [256], replicated
- grad_theta_log: float32 [256], replicated
- grad_c_proj: float32 [512, 512], replicated
- grad_d_skip: float32 [512], replicated
- grad_glu_weight: float32 [512, 1024], replicated
The draws below stay inside these ranges and needn't reach their ends.
Inputs may be any that keep to these rules, and one draw needn't show every extreme that they name: `bucket_id`: bucket 0 is 128 tokens, bucket 1 is 512 tokens, bucket 2 is 2048 tokens; a run of equal ids covers whole aligned runs of that bucket's length; pattern 0 of every group is bucket 2 throughout, the others hold buckets 0 and 1. `assignment`: in each group every pattern is held by exactly one lane.
All inputs are finite; a program needn't handle non-finite values.
Results may differ from the reference program's by a relative error of at most 0.012.
Values sent between devices are 32-bit elements; how exact they have to be, the bound alone decides.
No kernel may reach another device: no remote copies, remote signals or barrier semaphores. Data moves between devices by JAX's collectives and lax.ppermute only.
A program may use at most 128 MiB of HBM per device.

```python
import jax
import jax.numpy as jnp
from jax import lax

H = 512
STATES = 256
LANES = 4
BLOCKS = 16
GROUPS = 4
LONG = 2048
SHORT = 128


def decay_rates(key, share):
    pick_key = jax.random.fold_in(key, 101)
    slow_key = jax.random.fold_in(key, 102)
    fast_key = jax.random.fold_in(key, 103)
    slow = jax.random.bernoulli(pick_key, share, (STATES,))
    slow_rate = jnp.exp(jnp.log(0.2 / LONG) + jax.random.uniform(slow_key, (STATES,), jnp.float32) * jnp.log(10.0))
    fast_rate = jnp.exp(jnp.log(0.02) + jax.random.uniform(fast_key, (STATES,), jnp.float32) * jnp.log(2.5))
    return jnp.where(slow, slow_rate, fast_rate)


def draw_nu_log(key, part):
    share = 0.5
    rates = decay_rates(key, share)
    return jnp.log(rates).astype(jnp.float32)


def draw_gamma_log(key, part):
    share = 0.5
    rates = decay_rates(key, share)
    key = jax.random.fold_in(key, 7)
    jitter = jax.random.uniform(key, (STATES,), jnp.float32, -0.3, 0.3)
    return (0.5 * jnp.log(1.0 - jnp.exp(-2.0 * rates)) + jitter).astype(jnp.float32)


def draw_bucket_id(key, part):
    key = jax.random.fold_in(key, 5)
    quarters = jax.random.randint(key, (GROUPS, LANES, 4), 0, 2)
    ids = jnp.repeat(quarters, BLOCKS // 4, axis=2)
    ids = ids.at[:, 0, :].set(2)
    return ids.astype(jnp.int32)


def levels(own_key, shape, split, smallest, high):
    loudness = 1.0
    for dim, parts in split:
        steps = jax.random.uniform(jax.random.fold_in(jax.random.fold_in(own_key, 6), dim), (parts,), jnp.float32, smallest / len(split), high / len(split))
        loudness = loudness * jnp.repeat(jnp.exp(steps), shape[dim] // parts).reshape((-1,) + (1,) * (len(shape) - 1 - dim))
    return loudness


def normal_values(own_key, extent, spread, reach, split=(), kind=jnp.bfloat16):
    level = levels(own_key, extent, split, -0.22, 0.18) if split else 1.0
    drawn = jax.random.normal(own_key, extent, jnp.float32) * spread * level
    return jnp.minimum(jnp.maximum(drawn, -reach), reach).astype(kind)


def setup_inputs(seed: int = 0) -> dict:
    arg_keys = jax.random.split(jax.random.key(seed), 13)
    block_in = normal_values(arg_keys[0], (GROUPS, LANES, LONG, H), 1.0, 6.0, ((0, 4), (2, 8)))
    cotangent = normal_values(arg_keys[1], (GROUPS, LANES, LONG, H), 1.0, 6.0, ((0, 4), (2, 8)))
    bucket_id = draw_bucket_id(jax.random.fold_in(arg_keys[12], 71), 0)
    assignment = jax.vmap(lambda own: jax.random.permutation(own, LANES))(jax.random.split(arg_keys[3], GROUPS)).reshape((GROUPS, LANES)).astype(jnp.int32)
    norm_gain = jnp.clip(1.0 + 0.15 * jax.random.normal(arg_keys[4], (H,), jnp.float32), 0.25, 1.75)
    b_proj = normal_values(arg_keys[5], (H, 2 * STATES), H ** -0.5, 0.25)
    gamma_log = draw_gamma_log(jax.random.fold_in(arg_keys[12], 71), 0)
    nu_log = draw_nu_log(jax.random.fold_in(arg_keys[12], 71), 0)
    theta_log = jnp.clip(jax.random.uniform(arg_keys[8], (STATES,), jnp.float32, -6.9, 1.1), -6.9, 1.1)
    c_proj = normal_values(arg_keys[9], (2 * STATES, H), STATES ** -0.5, 0.375)
    d_skip = normal_values(arg_keys[10], (H,), 1.0, 4.0, (), jnp.float32)
    glu_weight = normal_values(arg_keys[11], (H, 2 * H), H ** -0.5, 0.25)
    return {"block_in": block_in, "cotangent": cotangent, "bucket_id": bucket_id, "assignment": assignment, "norm_gain": norm_gain, "b_proj": b_proj, "gamma_log": gamma_log, "nu_log": nu_log, "theta_log": theta_log, "c_proj": c_proj, "d_skip": d_skip, "glu_weight": glu_weight}


EPS = 1e-05

@jax.custom_vjp
def low(v):
    return lax.optimization_barrier(v.astype(jnp.bfloat16)).astype(jnp.float32)

@jax.custom_vjp
def low_back(v):
    return v

def low_keep(v):
    return (low(v), None)

def low_pass(kept, grad):
    return (grad,)

def back_keep(v):
    return (v, None)

def back_low(kept, grad):
    return (low(grad),)
low.defvjp(low_keep, low_pass)
low_back.defvjp(back_keep, back_low)

def join(early, late):
    e_re, e_im, f_re, f_im = early
    l_re, l_im, g_re, g_im = late
    return (e_re * l_re - e_im * l_im, e_re * l_im + e_im * l_re, l_re * f_re - l_im * f_im + g_re, l_re * f_im + l_im * f_re + g_im)

def lane_forward(params, rows, start):
    gain, b_mat, g_log, nu_par, th_par, c_mat, d_vec, w_glu = params
    mean_row = lax.optimization_barrier(jnp.mean(rows, axis=-1, keepdims=True))
    centred = rows - mean_row
    var_row = lax.optimization_barrier(jnp.mean(centred * centred, axis=-1, keepdims=True))
    normed = low(centred * lax.rsqrt(var_row + EPS) * gain)
    b_out = low_back(jnp.dot(normed, b_mat, precision=lax.Precision.HIGHEST))
    factor = jnp.exp(g_log)
    driven = b_out * jnp.concatenate([factor, factor])
    modulus = jnp.exp(-jnp.exp(nu_par))
    phase = jnp.exp(th_par)
    lam_re = modulus * jnp.cos(phase)
    lam_im = modulus * jnp.sin(phase)
    a_re = jnp.where(start[:, None], 0.0, lam_re[None, :])
    a_im = jnp.where(start[:, None], 0.0, lam_im[None, :])
    scanned = lax.associative_scan(join, (a_re, a_im, driven[:, :STATES], driven[:, STATES:]), axis=0)
    states = low(jnp.concatenate([scanned[2], scanned[3]], axis=-1))
    c_out = low_back(jnp.dot(states, c_mat, precision=lax.Precision.HIGHEST))
    mixed = c_out + d_vec * normed
    gelu_out = low(jax.nn.gelu(mixed, approximate=True))
    pre_glu = low_back(jnp.dot(gelu_out, w_glu, precision=lax.Precision.HIGHEST))
    gated = pre_glu[:, :H] * jax.nn.sigmoid(pre_glu[:, H:])
    return rows + gated

def reference(block_in, cotangent, bucket_id, assignment, norm_gain, b_proj, gamma_log, nu_log, theta_log, c_proj, d_skip, glu_weight):
    params = tuple((v.astype(jnp.float32) for v in (norm_gain, b_proj, gamma_log, nu_log, theta_log, c_proj, d_skip, glu_weight)))
    chosen = jnp.broadcast_to(assignment[:, :, None].astype(jnp.int32), bucket_id.shape)
    patterns = jnp.take_along_axis(bucket_id, chosen, axis=1)
    position = jnp.arange(LONG, dtype=jnp.int32)
    block_of = position // SHORT
    bucket_rows = patterns[:, :, block_of]
    span = SHORT * jnp.where(bucket_rows == 0, 1, jnp.where(bucket_rows == 1, 4, 16))
    starts = position[None, None, :] % span == 0
    flat_in = block_in.reshape(GROUPS * LANES, LONG, H)
    flat_cot = cotangent.reshape(GROUPS * LANES, LONG, H)
    flat_start = starts.reshape(GROUPS * LANES, LONG)
    zero_grads = tuple((jnp.zeros_like(v) for v in params))

    def one_lane(totals, item):
        rows, cot, start = item
        result, pull = jax.vjp(lambda prm, val: lane_forward(prm, val, start), params, rows.astype(jnp.float32))
        grad_params, grad_rows = pull(cot.astype(jnp.float32))
        totals = tuple((a_tot + b_new for a_tot, b_new in zip(totals, grad_params)))
        return (totals, (result.astype(jnp.bfloat16), grad_rows.astype(jnp.bfloat16)))
    totals, (outs, grads) = lax.scan(one_lane, zero_grads, (flat_in, flat_cot, flat_start))
    block_out = outs.reshape(GROUPS, LANES, LONG, H)
    grad_in = grads.reshape(GROUPS, LANES, LONG, H)
    return (block_out, grad_in, totals[0], totals[1], totals[2], totals[3], totals[4], totals[5], totals[6], totals[7])
```

```python
import functools

import jax
import jax.numpy as jnp
from jax import lax
from jax.experimental import pallas as pl
from jax.experimental.pallas import tpu as pltpu
from jax.sharding import PartitionSpec as P

EPS = 1e-05
CHUNKS = 8
LANE = 128
GELU_A = 0.044715
GELU_K = 0.7978845608028654
VMEM = 56 * 1024 * 1024
F32 = jnp.float32
BF16 = jnp.bfloat16


def dot_nt(left, right):
    return lax.dot_general(left, right, (((1,), (1,)), ((), ())), preferred_element_type=F32)


def dot_tn(left, right):
    return lax.dot_general(left, right, (((0,), (0,)), ((), ())), preferred_element_type=F32)


def dot_nn(left, right):
    return jnp.dot(left, right, preferred_element_type=F32)


def cmul(x, y):
    return x[0] * y[0] - x[1] * y[1], x[0] * y[1] + x[1] * y[0]


def cadd(x, y):
    return x[0] + y[0], x[1] + y[1]


def conj(x):
    return x[0], -x[1]


def pair_rows(ref, row, count=1):
    pairs = ref.shape[1] // (2 * LANE)
    cut = [ref[row : row + count, k * LANE : (k + 1) * LANE] for k in range(2 * pairs)]
    return list(zip(cut[:pairs], cut[pairs:]))


def load_pairs(ref, step, span):
    pairs = ref.shape[0] // 2
    cut = [ref[k, pl.ds(step, CHUNKS, stride=span), :] for k in range(2 * pairs)]
    return list(zip(cut[:pairs], cut[pairs:]))


def store_pairs(ref, step, span, values):
    pairs = ref.shape[0] // 2
    for k, (re, im) in enumerate(values):
        ref[k, pl.ds(step, CHUNKS, stride=span), :] = re
        ref[pairs + k, pl.ds(step, CHUNKS, stride=span), :] = im


def join_pairs(values):
    return jnp.concatenate([v[0] for v in values], 1), jnp.concatenate([v[1] for v in values], 1)


def put_blocks(ref, value):
    for k in range(ref.shape[0]):
        ref[k] = value[:, k * LANE : (k + 1) * LANE]


def get_blocks(ref):
    return jnp.concatenate([ref[k] for k in range(ref.shape[0])], 1)


def keeps(bucket, assign, own, lane, seg, short):
    pattern = assign[lane]
    found = []
    for chunk in range(CHUNKS):
        token = own[0] * seg + chunk * (seg // CHUNKS)
        bucket_here = bucket[pattern, lax.div(token, short)]
        span = jnp.where(bucket_here == 0, short, jnp.where(bucket_here == 1, 4 * short, 16 * short))
        found.append(jnp.where(lax.rem(token, span) == 0, 0.0, 1.0).astype(F32))
    return found


def norm_stats(rows):
    mean = jnp.mean(rows, axis=-1, keepdims=True)
    centred = rows - mean
    var = jnp.mean(centred * centred, axis=-1, keepdims=True)
    scale = lax.rsqrt(var + EPS)
    return centred * scale, scale


def halves(value, n):
    return value[:, :n], value[:, n:]


def first_kernel(
    short, bucket, assign, own, x_ref, gain_ref, b_ref, gamma_ref, nu_ref, th_ref,
    normed_ref, loc_ref, ends_ref, total_ref, decay_ref, pow_ref, u_ref,
):
    seg = x_ref.shape[0]
    n = nu_ref.shape[1]
    span = seg // CHUNKS
    lane = pl.program_id(0)

    @pl.when(lane == 0)
    def _():
        modulus = jnp.exp(-jnp.exp(nu_ref[...]))
        phase = jnp.exp(th_ref[...])
        pow_ref[0:1, :n] = modulus * jnp.cos(phase)
        pow_ref[0:1, n:] = modulus * jnp.sin(phase)
        size = 1
        while size < span:
            low = pow_ref[0:size, :n], pow_ref[0:size, n:]
            top = pow_ref[size - 1 : size, :n], pow_ref[size - 1 : size, n:]
            re, im = cmul(low, top)
            pow_ref[size : 2 * size, :n] = re
            pow_ref[size : 2 * size, n:] = im
            size *= 2

    xhat, _ = norm_stats(x_ref[...].astype(F32))
    low = (xhat * gain_ref[...]).astype(BF16)
    normed_ref[...] = low
    factor = jnp.exp(gamma_ref[...])
    b_out = dot_nn(low, b_ref[...])
    put_blocks(u_ref, jnp.concatenate([b_out[:, :n] * factor, b_out[:, n:] * factor], 1))

    lam = pair_rows(pow_ref, 0)
    h = None
    for step in range(span):
        u = load_pairs(u_ref, step, span)
        h = u if h is None else [cadd(cmul(a, x), v) for a, x, v in zip(lam, h, u)]
        store_pairs(loc_ref, step, span, h)
    h = join_pairs(h)
    ends_ref[:, :n] = h[0]
    ends_ref[:, n:] = h[1]

    keep = keeps(bucket, assign, own, lane, seg, short)
    lam_span = pow_ref[span - 1 : span, :n], pow_ref[span - 1 : span, n:]
    state = h[0][0:1], h[1][0:1]
    decay = lam_span[0] * keep[0], lam_span[1] * keep[0]
    for chunk in range(1, CHUNKS):
        step = lam_span[0] * keep[chunk], lam_span[1] * keep[chunk]
        re, im = cmul(step, state)
        state = re + h[0][chunk : chunk + 1], im + h[1][chunk : chunk + 1]
        decay = cmul(step, decay)
    total_ref[:, :n], total_ref[:, n:] = state
    decay_ref[:, :n], decay_ref[:, n:] = decay


def middle_kernel(
    short, bucket, assign, own, x_ref, ct_ref, normed_ref, loc_ref, ends_ref, enter_ref, pow_ref,
    c_ref, d_ref, w_ref,
    out_ref, h_ref, carry_ref, adj_ref, firsts_ref, back_ref, mixed_ref, g_w_ref, g_c_ref, g_d_ref,
    g_ref,
):
    seg, width = x_ref.shape
    n = c_ref.shape[0] // 2
    span = seg // CHUNKS
    lane = pl.program_id(0)
    keep = keeps(bucket, assign, own, lane, seg, short)
    lam_span = pow_ref[span - 1 : span, :n], pow_ref[span - 1 : span, n:]

    entry = enter_ref[pl.ds(lane, 1), :]
    state = entry[:, :n] * keep[0], entry[:, n:] * keep[0]
    carry_ref[0:1, :n], carry_ref[0:1, n:] = state
    for chunk in range(1, CHUNKS):
        re, im = cmul(lam_span, state)
        state = (
            (re + ends_ref[chunk - 1 : chunk, :n]) * keep[chunk],
            (im + ends_ref[chunk - 1 : chunk, n:]) * keep[chunk],
        )
        carry_ref[chunk : chunk + 1, :n], carry_ref[chunk : chunk + 1, n:] = state
    carry = pair_rows(carry_ref, 0, CHUNKS)
    for step in range(span):
        loc = load_pairs(loc_ref, step, span)
        power = pair_rows(pow_ref, step)
        store_pairs(h_ref, step, span, [cadd(v, cmul(a, x)) for a, x, v in zip(power, carry, loc)])

    states = get_blocks(h_ref).astype(BF16)
    normed = normed_ref[...].astype(F32)
    mixed = dot_nn(states, c_ref[...]) + d_ref[...] * normed
    square = mixed * mixed
    tanh = jnp.tanh(GELU_K * mixed * (1.0 + GELU_A * square))
    half_up = 0.5 * (1.0 + tanh)
    gelu = (mixed * half_up).astype(BF16)
    slope = half_up + 0.5 * GELU_K * mixed * (1.0 - tanh * tanh) * (1.0 + 3.0 * GELU_A * square)
    pre = dot_nn(gelu, w_ref[...])
    value = pre[:, :width]
    sig = jax.nn.sigmoid(pre[:, width:])
    gated = value * sig
    out_ref[...] = (x_ref[...].astype(F32) + gated).astype(BF16)
    cot = ct_ref[...].astype(F32)
    first = cot * sig
    pre_low = jnp.concatenate([first, first * (value - gated)], axis=1).astype(BF16)

    @pl.when(lane == 0)
    def _():
        g_w_ref[...] = jnp.zeros_like(g_w_ref)
        g_c_ref[...] = jnp.zeros_like(g_c_ref)
        g_d_ref[...] = jnp.zeros_like(g_d_ref)

    g_w_ref[...] += dot_tn(gelu, pre_low)
    grad_mixed = dot_nt(pre_low, w_ref[...]) * slope
    mixed_ref[...] = grad_mixed
    g_d_ref[...] += jnp.sum(grad_mixed * normed, axis=0, keepdims=True)
    low = grad_mixed.astype(BF16)
    g_c_ref[...] += dot_tn(states, low)
    put_blocks(g_ref, dot_nt(low, c_ref[...]))

    lam = [conj(a) for a in pair_rows(pow_ref, 0)]
    adj = None
    for step in reversed(range(span)):
        g = load_pairs(g_ref, step, span)
        adj = g if adj is None else [cadd(cmul(a, x), v) for a, x, v in zip(lam, adj, g)]
        store_pairs(adj_ref, step, span, adj)
    adj = join_pairs(adj)
    firsts_ref[:, :n], firsts_ref[:, n:] = adj
    back = lam_span[0], -lam_span[1]
    state = adj[0][CHUNKS - 1 :] * keep[CHUNKS - 1], adj[1][CHUNKS - 1 :] * keep[CHUNKS - 1]
    for chunk in reversed(range(CHUNKS - 1)):
        re, im = cmul(back, state)
        state = (
            (re + adj[0][chunk : chunk + 1]) * keep[chunk],
            (im + adj[1][chunk : chunk + 1]) * keep[chunk],
        )
    back_ref[:, :n], back_ref[:, n:] = state


def last_kernel(
    short, bucket, assign, own, x_ref, ct_ref, normed_ref, h_ref, carry_ref, adj_ref, firsts_ref,
    leave_ref, mixed_ref, pow_ref, gain_ref, b_ref, gamma_ref, d_ref, g_d_ref,
    in_ref, g_b_ref, small_ref, back_ref, after_ref, lam_ref,
):
    seg, width = x_ref.shape
    n = gamma_ref.shape[1]
    span = seg // CHUNKS
    lane = pl.program_id(0)
    keep = keeps(bucket, assign, own, lane, seg, short)
    back = pow_ref[span - 1 : span, :n], -pow_ref[span - 1 : span, n:]

    @pl.when(lane == 0)
    def _():
        g_b_ref[...] = jnp.zeros_like(g_b_ref)
        lam_ref[...] = jnp.zeros_like(lam_ref)

    entry = leave_ref[pl.ds(lane, 1), :]
    state = entry[:, :n], entry[:, n:]
    rows = [state]
    for chunk in reversed(range(1, CHUNKS)):
        re, im = cmul(back, state)
        state = (
            (re + firsts_ref[chunk : chunk + 1, :n]) * keep[chunk],
            (im + firsts_ref[chunk : chunk + 1, n:]) * keep[chunk],
        )
        rows.append(state)
    rows.reverse()
    for chunk, state in enumerate(rows):
        after_ref[chunk : chunk + 1, :n], after_ref[chunk : chunk + 1, n:] = state
    after = pair_rows(after_ref, 0, CHUNKS)
    factor = jnp.exp(gamma_ref[...])
    factor = jnp.concatenate([factor, factor], 1)
    scale = pair_rows(factor, 0)
    sums = None
    before = pair_rows(carry_ref, 0, CHUNKS)
    for step in range(span):
        power = [conj(a) for a in pair_rows(pow_ref, span - 1 - step)]
        local = load_pairs(adj_ref, step, span)
        full = [cadd(v, cmul(a, x)) for a, x, v in zip(power, after, local)]
        add = [cmul(conj(x), v) for x, v in zip(before, full)]
        sums = add if sums is None else [cadd(x, v) for x, v in zip(sums, add)]
        store_pairs(back_ref, step, span, [(v[0] * a[0], v[1] * a[0]) for a, v in zip(scale, full)])
        before = load_pairs(h_ref, step, span)
    sums = join_pairs(sums)
    lam_ref[:, :n] += sums[0]
    lam_ref[:, n:] += sums[1]

    back_low = get_blocks(back_ref).astype(BF16)
    g_b_ref[...] += dot_tn(normed_ref[...], back_low)
    grad_normed = dot_nt(back_low, b_ref[...]) + mixed_ref[...] * d_ref[...]
    xhat, scale = norm_stats(x_ref[...].astype(F32))
    dxhat = grad_normed * gain_ref[...]
    one = jnp.mean(dxhat, axis=-1, keepdims=True)
    two = jnp.mean(dxhat * xhat, axis=-1, keepdims=True)
    in_ref[...] = (ct_ref[...].astype(F32) + (dxhat - one - xhat * two) * scale).astype(BF16)

    @pl.when(lane == pl.num_programs(0) - 1)
    def _():
        prod = g_b_ref[...] * b_ref[...].astype(F32)
        small_ref[...] = jnp.zeros_like(small_ref)
        small_ref[0:1, :] = jnp.sum(lam_ref[...], axis=0, keepdims=True)
        small_ref[1:2, :] = jnp.sum(prod, axis=0, keepdims=True)
        small_ref[2:3, :] = jnp.sum(prod.T, axis=0, keepdims=True) + d_ref[...] * g_d_ref[...]
        small_ref[3:4, :] = g_d_ref[...]


def swap(value, axis, bit):
    count = lax.axis_size(axis)
    return lax.ppermute(value, axis, [(i, i ^ (1 << bit)) for i in range(count)])


def entering(total, decay, n, backward):
    def mul(x, y):
        return jnp.concatenate(
            [x[:, :n] * y[:, :n] - x[:, n:] * y[:, n:], x[:, :n] * y[:, n:] + x[:, n:] * y[:, :n]], 1
        )

    count, mine = lax.axis_size("seq"), lax.axis_index("seq")
    prefix = jnp.zeros_like(total)
    through = jnp.concatenate([jnp.ones_like(total[:, :n]), jnp.zeros_like(total[:, n:])], 1)
    for bit in range(count.bit_length() - 1):
        got = swap(jnp.stack([total, decay]), "seq", bit)
        other, other_decay = got[0], got[1]
        later = (lax.div(mine, 1 << bit) % 2 == 1) != backward
        prefix = jnp.where(later, prefix + mul(through, other), prefix)
        through = jnp.where(later, mul(through, other_decay), through)
        total = jnp.where(later, total + mul(decay, other), other + mul(other_decay, total))
        decay = mul(decay, other_decay)
    return prefix


def on_device(
    block_in, cotangent, bucket_id, assignment, norm_gain, b_proj, gamma_log, nu_log, theta_log,
    c_proj, d_skip, glu_weight,
):
    _, lanes, seg, width = block_in.shape
    n = nu_log.shape[0]
    two = 2 * n
    short = seg * lax.axis_size("seq") // bucket_id.shape[2]
    span = seg // CHUNKS
    blocks = two // LANE
    own = lax.axis_index("seq").astype(jnp.int32).reshape(1)
    scalars = (bucket_id[0], assignment[0], own)

    def row(v):
        return v.reshape(1, -1)

    smem = [pl.BlockSpec(memory_space=pltpu.SMEM)] * 3
    big = pl.BlockSpec((None, None, seg, width), lambda l: (0, l, 0, 0))
    tokens = pl.BlockSpec((None, seg, width), lambda l: (l, 0, 0))
    states = pl.BlockSpec((None, blocks, seg, LANE), lambda l: (l, 0, 0, 0))
    chunk_rows = pl.BlockSpec((None, CHUNKS, two), lambda l: (l, 0, 0))
    lane_row = pl.BlockSpec((None, 1, two), lambda l: (l, 0, 0))

    def whole(*shape):
        return pl.BlockSpec(shape, lambda l: (0,) * len(shape))

    def out(shape, kind=F32):
        return jax.ShapeDtypeStruct(shape, kind)

    params = pltpu.CompilerParams(vmem_limit_bytes=VMEM)

    normed, loc, ends, total, decay, powers = pl.pallas_call(
        functools.partial(first_kernel, short),
        grid=(lanes,),
        in_specs=smem + [big, whole(1, width), whole(width, two), whole(1, n), whole(1, n), whole(1, n)],
        out_specs=[tokens, states, chunk_rows, lane_row, lane_row, whole(span, two)],
        out_shape=[
            out((lanes, seg, width), BF16), out((lanes, blocks, seg, LANE)), out((lanes, CHUNKS, two)),
            out((lanes, 1, two)), out((lanes, 1, two)), out((span, two)),
        ],
        scratch_shapes=[pltpu.VMEM((blocks, seg, LANE), F32)],
        compiler_params=params,
        name="forward_local",
    )(*scalars, block_in, row(norm_gain), b_proj, row(gamma_log), row(nu_log), row(theta_log))

    total, decay = total[:, 0], decay[:, 0]
    enter = entering(total, decay, n, False)

    block_out, h, carry, adj, firsts, back_total, grad_mixed, grad_w, grad_c, grad_d = pl.pallas_call(
        functools.partial(middle_kernel, short),
        grid=(lanes,),
        in_specs=smem + [
            big, big, tokens, states, chunk_rows, whole(lanes, two), whole(span, two),
            whole(two, width), whole(1, width), whole(width, 2 * width),
        ],
        out_specs=[
            big, states, chunk_rows, states, chunk_rows, lane_row, tokens,
            whole(width, 2 * width), whole(two, width), whole(1, width),
        ],
        out_shape=[
            out(block_in.shape, BF16), out((lanes, blocks, seg, LANE)), out((lanes, CHUNKS, two)),
            out((lanes, blocks, seg, LANE)), out((lanes, CHUNKS, two)), out((lanes, 1, two)),
            out((lanes, seg, width)), out((width, 2 * width)), out((two, width)), out((1, width)),
        ],
        scratch_shapes=[pltpu.VMEM((blocks, seg, LANE), F32)],
        compiler_params=params,
        name="block_and_back",
    )(*scalars, block_in, cotangent, normed, loc, ends, enter, powers, c_proj, row(d_skip), glu_weight)

    conj = jnp.concatenate([decay[:, :n], -decay[:, n:]], 1)
    leave = entering(back_total[:, 0], conj, n, True)

    grad_in, grad_b, small = pl.pallas_call(
        functools.partial(last_kernel, short),
        grid=(lanes,),
        in_specs=smem + [
            big, big, tokens, states, chunk_rows, states, chunk_rows, whole(lanes, two), tokens,
            whole(span, two), whole(1, width), whole(width, two), whole(1, n), whole(1, width),
            whole(1, width),
        ],
        out_specs=[big, whole(width, two), whole(8, two)],
        out_shape=[out(block_in.shape, BF16), out((width, two)), out((8, two))],
        scratch_shapes=[
            pltpu.VMEM((blocks, seg, LANE), F32), pltpu.VMEM((CHUNKS, two), F32),
            pltpu.VMEM((CHUNKS, two), F32),
        ],
        compiler_params=params,
        name="back_last",
    )(
        *scalars, block_in, cotangent, normed, h, carry, adj, firsts, leave, grad_mixed, powers,
        row(norm_gain), b_proj, row(gamma_log), row(d_skip), grad_d,
    )

    grad_w, grad_c, grad_b, small = lax.psum((grad_w, grad_c, grad_b, small), ("dp", "seq"))
    lam_re, lam_im = powers[0, :n], powers[0, n:]
    p, q = small[0, :n], small[0, n:]
    grad_nu = -jnp.exp(nu_log) * (p * lam_re + q * lam_im)
    grad_theta = -jnp.exp(theta_log) * (p * lam_im - q * lam_re)
    grad_gamma = small[1, :n] + small[1, n:]
    grad_gain = small[2] / norm_gain
    return (
        block_out, grad_in, grad_gain, grad_b, grad_gamma, grad_nu, grad_theta, grad_c, small[3],
        grad_w,
    )


def solution(mesh):
    rows = P("dp", None, "seq", None)
    in_specs = (rows, rows, P("dp", None, None), P("dp", None)) + (P(),) * 8
    out_specs = (rows, rows) + (P(),) * 8
    return jax.shard_map(
        on_device, mesh=mesh, in_specs=in_specs, out_specs=out_specs, check_vma=False
    )
```

```python
import functools

import jax
import jax.numpy as jnp
from jax import lax
from jax.experimental import pallas as pl
from jax.experimental.pallas import tpu as pltpu
from jax.sharding import PartitionSpec as P

EPS = 1e-05
CHUNKS = 8
LANE = 128
GELU_A = 0.044715
GELU_K = 0.7978845608028654
F32 = jnp.float32
BF16 = jnp.bfloat16


def dot_nt(left, right):
    return lax.dot_general(left, right, (((1,), (1,)), ((), ())), preferred_element_type=F32)


def dot_tn(left, right):
    return lax.dot_general(left, right, (((0,), (0,)), ((), ())), preferred_element_type=F32)


def dot_nn(left, right):
    return jnp.dot(left, right, preferred_element_type=F32)


def cmul(x, y):
    return x[0] * y[0] - x[1] * y[1], x[0] * y[1] + x[1] * y[0]


def cadd(x, y):
    return x[0] + y[0], x[1] + y[1]


def fma(a, x, y):
    return (y[0] - a[1] * x[1]) + a[0] * x[0], (y[1] + a[1] * x[0]) + a[0] * x[1]


def conj(x):
    return x[0], -x[1]


def cload(ref, first, count=1):
    n = ref.shape[-1] // 2
    return ref[first : first + count, :n], ref[first : first + count, n:]


def cstore(ref, first, value):
    n = ref.shape[-1] // 2
    rows = value[0].shape[0]
    ref[first : first + rows, :n], ref[first : first + rows, n:] = value


def kept(ref, row, value):
    keep = cload(ref, row)
    return value[0] * keep[0], value[1] * keep[1]


def scan_order(seg, back=False):
    row = lax.broadcasted_iota(jnp.int32, (seg, seg), 0)
    column = lax.broadcasted_iota(jnp.int32, (seg, seg), 1)
    if back:
        row, column = column, row
    span = seg // CHUNKS
    hit = (row % CHUNKS == column // span) & (row // CHUNKS == column % span)
    return jnp.where(hit, 1.0, 0.0).astype(BF16)


def fill_keeps(bucket, assign, keep_ref, lanes, seg, short):
    own = lax.axis_index("seq")
    for lane in range(lanes):
        pattern = assign[0, lane]
        for chunk in range(CHUNKS):
            token = own * seg + chunk * (seg // CHUNKS)
            here = bucket[pattern, lax.div(token, short)]
            span = jnp.where(here == 0, short, jnp.where(here == 1, 4 * short, 16 * short))
            keep = jnp.where(lax.rem(token, span) == 0, 0.0, 1.0).astype(F32)
            row = lane * CHUNKS + chunk
            keep_ref[row : row + 1, :] = jnp.full((1, keep_ref.shape[1]), keep)


def norm_stats(rows):
    mean = jnp.mean(rows, axis=-1, keepdims=True)
    centred = rows - mean
    var = jnp.mean(centred * centred, axis=-1, keepdims=True)
    scale = lax.rsqrt(var + EPS)
    return centred * scale, scale


def cost(micros):
    return pl.CostEstimate(flops=int(micros * 1.1e9), bytes_accessed=int(micros * 3e6), transcendentals=0)


def put_halves(value, keep, send):
    rows = value.shape[0] // 2
    first = lax.rem(lax.axis_index("seq"), 2) == 0
    top, bottom = value[:rows], value[rows:]
    keep[...] = jnp.where(first, top, bottom)
    send[...] = jnp.where(first, bottom, top)


class Copies:
    def __init__(self, sems):
        self.sems, self.all = sems, []

    def start(self, source, target):
        copy = pltpu.make_async_copy(source, target, self.sems.at[len(self.all)])
        copy.start()
        self.all.append(copy)
        return copy

    def lanes(self, lanes, *pairs):
        return [
            [self.start(lane_of(source, lane, lanes), lane_of(target, lane, lanes)) for source, target in pairs]
            for lane in range(lanes)
        ]


def lane_of(ref, lane, lanes):
    if len(ref.shape) == 3:
        return ref.at[lane]
    rows = ref.shape[0] // lanes
    return ref.at[pl.ds(lane * rows, rows)]


def wait(copies):
    for copy in copies:
        copy.wait()


def first_kernel(
    short, bucket_hbm, assign_hbm, x_hbm, gain_hbm, b_hbm, gamma_hbm, nu_hbm, th_hbm,
    xs_hbm, normed_hbm, loc_hbm, pair_ref, pow_ref, keep_ref,
    bucket, assign, x_ref, gain_ref, b_ref, gamma_ref, nu_ref, th_ref, xs_ref, normed_ref, loc_ref, sems,
):
    lanes, seg, width = x_ref.shape
    span = seg // CHUNKS
    copies = Copies(sems)
    x_here = copies.lanes(lanes, (x_hbm, x_ref))
    nu_here, th_here = copies.start(nu_hbm, nu_ref), copies.start(th_hbm, th_ref)
    gain_here, gamma_here = copies.start(gain_hbm, gain_ref), copies.start(gamma_hbm, gamma_ref)
    b_here = copies.start(b_hbm, b_ref)
    tables = copies.start(bucket_hbm, bucket), copies.start(assign_hbm, assign)
    leaving = []

    order = scan_order(seg)
    nu_here.wait(), th_here.wait()
    modulus = jnp.exp(-jnp.exp(nu_ref[...]))
    phase = jnp.exp(th_ref[...])
    cstore(pow_ref, 0, (modulus * jnp.cos(phase), modulus * jnp.sin(phase)))
    size = 1
    while size < span:
        cstore(pow_ref, size, cmul(cload(pow_ref, 0, size), cload(pow_ref, size - 1)))
        size *= 2

    gain_here.wait(), gamma_here.wait()
    factor = jnp.exp(gamma_ref[...])
    factor = jnp.concatenate([factor, factor], 1)
    for lane in range(lanes):
        rows = pl.ds(lane * seg, seg)
        wait(x_here[lane])
        x = dot_nn(order, x_ref[lane])
        xs_ref[rows, :] = x.astype(BF16)
        xhat, _ = norm_stats(x)
        low = (xhat * gain_ref[...]).astype(BF16)
        normed_ref[rows, :] = low
        if lane == 0:
            b_here.wait()
        loc_ref[rows, :] = dot_nn(low, b_ref[...]) * factor
        for source, target in ((xs_ref, xs_hbm), (normed_ref, normed_hbm)):
            leaving.append(copies.start(source.at[rows], target.at[rows]))

    for table in tables:
        table.wait()
    fill_keeps(bucket, assign, keep_ref, lanes, seg, short)
    lam = cload(pow_ref, 0)
    lam_span = cload(pow_ref, span - 1)
    for lane in range(lanes):
        h = cload(loc_ref, lane * seg, CHUNKS)
        for step in range(1, span):
            at = lane * seg + step * CHUNKS
            h = fma(lam, h, cload(loc_ref, at, CHUNKS))
            cstore(loc_ref, at, h)
        rows = pl.ds(lane * seg, seg)
        leaving.append(copies.start(loc_ref.at[rows], loc_hbm.at[rows]))
        state = h[0][0:1], h[1][0:1]
        decay = kept(keep_ref, lane * CHUNKS, lam_span)
        for chunk in range(1, CHUNKS):
            step = kept(keep_ref, lane * CHUNKS + chunk, lam_span)
            state = fma(step, state, (h[0][chunk : chunk + 1], h[1][chunk : chunk + 1]))
            decay = cmul(step, decay)
        cstore(pair_ref, lane, state)
        cstore(pair_ref, lanes + lane, decay)
    wait(leaving)


def block_kernel(
    ct_hbm, c_hbm, d_hbm, w_hbm, xs_hbm, normed_hbm, loc_hbm, enter_ref, pow_ref, keep_ref,
    out_hbm, cts_hbm, h_hbm, carry_ref, states_ref, slope_ref, pre_ref, go_ref, send_ref,
    ct_ref, c_ref, d_ref, w_ref, xs_ref, normed_ref, h_ref, out_ref, cts_ref, gelu_ref, sems,
):
    lanes, seg, width = ct_ref.shape
    copies = Copies(sems)
    loc_here = copies.lanes(lanes, (loc_hbm, h_ref))
    c_here, d_here = copies.start(c_hbm, c_ref), copies.start(d_hbm, d_ref)
    normed_here = copies.lanes(lanes, (normed_hbm, normed_ref))
    w_here = copies.start(w_hbm, w_ref)
    rest_here = copies.lanes(lanes, (xs_hbm, xs_ref), (ct_hbm, ct_ref))
    leaving = []
    span = seg // CHUNKS
    lam_span = cload(pow_ref, span - 1)
    order, order_back = scan_order(seg), scan_order(seg, True)
    for lane in range(lanes):
        first = lane * seg
        rows = pl.ds(first, seg)
        wait(loc_here[lane])
        last = first + (span - 1) * CHUNKS
        state = kept(keep_ref, lane * CHUNKS, cload(enter_ref, lane))
        cstore(carry_ref, lane * CHUNKS, state)
        for chunk in range(1, CHUNKS):
            state = fma(lam_span, state, cload(h_ref, last + chunk - 1))
            state = kept(keep_ref, lane * CHUNKS + chunk, state)
            cstore(carry_ref, lane * CHUNKS + chunk, state)
        carry = cload(carry_ref, lane * CHUNKS, CHUNKS)
        for step in range(span):
            at = first + step * CHUNKS
            cstore(h_ref, at, fma(cload(pow_ref, step), carry, cload(h_ref, at, CHUNKS)))
        leaving.append(copies.start(h_ref.at[rows], h_hbm.at[rows]))

        states = h_ref[rows, :].astype(BF16)
        states_ref[rows, :] = states
        if lane == 0:
            c_here.wait(), d_here.wait()
        wait(normed_here[lane])
        mixed = dot_nn(states, c_ref[...]) + d_ref[...] * normed_ref[rows, :].astype(F32)
        square = mixed * mixed
        tanh = jnp.tanh(GELU_K * mixed * (1.0 + GELU_A * square))
        half_up = 0.5 * (1.0 + tanh)
        gelu = (mixed * half_up).astype(BF16)
        gelu_ref[rows, :] = gelu
        slope_ref[rows, :] = half_up + 0.5 * GELU_K * mixed * (1.0 - tanh * tanh) * (
            1.0 + 3.0 * GELU_A * square
        )
        if lane == 0:
            w_here.wait()
        pre = dot_nn(gelu, w_ref[...])
        value = pre[:, :width]
        sig = jax.nn.sigmoid(pre[:, width:])
        gated = value * sig
        wait(rest_here[lane])
        out = (xs_ref[rows, :].astype(F32) + gated).astype(BF16)
        out_ref[lane] = dot_nn(order_back, out).astype(BF16)
        leaving.append(copies.start(out_ref.at[lane], out_hbm.at[lane]))
        cot = dot_nn(order, ct_ref[lane])
        cts_ref[rows, :] = cot.astype(BF16)
        leaving.append(copies.start(cts_ref.at[rows], cts_hbm.at[rows]))
        grad_value = cot * sig
        pre_ref[rows, :width] = grad_value.astype(BF16)
        pre_ref[rows, width:] = (grad_value * (value - gated)).astype(BF16)
    put_halves(dot_tn(gelu_ref[...], pre_ref[...]), go_ref, send_ref)
    wait(leaving)


def adjoint_kernel(
    w_hbm, c_hbm, normed_hbm, pre_ref, slope_ref, states_ref, pow_ref, keep_ref,
    mixed_hbm, adj_hbm, back_ref, g_d_ref, go_ref, send_ref,
    w_ref, c_ref, normed_ref, mixed_ref, adj_ref, low_ref, sems,
):
    copies = Copies(sems)
    w_here, c_here = copies.start(w_hbm, w_ref), copies.start(c_hbm, c_ref)
    normed_here = copies.lanes(back_ref.shape[0], (normed_hbm, normed_ref))
    leaving = []
    lanes = back_ref.shape[0]
    seg = pre_ref.shape[0] // lanes
    span = seg // CHUNKS
    lam, lam_span = conj(cload(pow_ref, 0)), conj(cload(pow_ref, span - 1))
    total = None
    w_here.wait()
    for lane in range(lanes):
        rows = pl.ds(lane * seg, seg)
        grad_mixed = dot_nt(pre_ref[rows, :], w_ref[...]) * slope_ref[rows, :]
        mixed_ref[rows, :] = grad_mixed
        leaving.append(copies.start(mixed_ref.at[rows], mixed_hbm.at[rows]))
        wait(normed_here[lane])
        add = jnp.sum(grad_mixed * normed_ref[rows, :].astype(F32), axis=0, keepdims=True)
        total = add if total is None else total + add
        low = grad_mixed.astype(BF16)
        low_ref[rows, :] = low
        if lane == 0:
            c_here.wait()
        adj_ref[rows, :] = dot_nt(low, c_ref[...])
    g_d_ref[...] = total
    for lane in range(lanes):
        adj = cload(adj_ref, (lane + 1) * seg - CHUNKS, CHUNKS)
        for step in reversed(range(span - 1)):
            at = lane * seg + step * CHUNKS
            adj = fma(lam, adj, cload(adj_ref, at, CHUNKS))
            cstore(adj_ref, at, adj)
        rows = pl.ds(lane * seg, seg)
        leaving.append(copies.start(adj_ref.at[rows], adj_hbm.at[rows]))
        state = None
        for chunk in reversed(range(CHUNKS)):
            here = adj[0][chunk : chunk + 1], adj[1][chunk : chunk + 1]
            state = here if state is None else fma(lam_span, state, here)
            state = kept(keep_ref, lane * CHUNKS + chunk, state)
        cstore(back_ref, lane, state)
    put_halves(dot_tn(states_ref[...], low_ref[...]), go_ref, send_ref)
    wait(leaving)


def states_kernel(
    b_hbm, gamma_hbm, d_hbm, normed_hbm, h_hbm, adj_hbm, leave_ref, carry_ref, pow_ref, keep_ref, g_d_ref,
    low_hbm, go_ref, send_ref, small_ref,
    b_ref, gamma_ref, d_ref, normed_ref, h_ref, adj_ref, low_ref, after_ref, sems,
):
    copies = Copies(sems)
    lanes_here = copies.lanes(leave_ref.shape[0], (adj_hbm, adj_ref), (h_hbm, h_ref))
    normed_here = copies.start(normed_hbm, normed_ref)
    leaving = []
    b_here, gamma_here, d_here = (
        copies.start(a, b) for a, b in ((b_hbm, b_ref), (gamma_hbm, gamma_ref), (d_hbm, d_ref))
    )
    lanes = leave_ref.shape[0]
    seg = normed_ref.shape[0] // lanes
    span = seg // CHUNKS
    back = conj(cload(pow_ref, span - 1))
    gamma_here.wait()
    factor = jnp.exp(gamma_ref[...])
    sums = None
    for lane in range(lanes):
        first = lane * seg
        state = cload(leave_ref, lane)
        wait(lanes_here[lane])
        cstore(after_ref, CHUNKS - 1, state)
        for chunk in reversed(range(1, CHUNKS)):
            state = fma(back, state, cload(adj_ref, first + chunk))
            state = kept(keep_ref, lane * CHUNKS + chunk, state)
            cstore(after_ref, chunk - 1, state)
        after = cload(after_ref, 0, CHUNKS)
        before = cload(carry_ref, lane * CHUNKS, CHUNKS)
        for step in range(span):
            at = first + step * CHUNKS
            full = fma(conj(cload(pow_ref, span - 1 - step)), after, cload(adj_ref, at, CHUNKS))
            add = cmul(conj(before), full)
            sums = add if sums is None else cadd(sums, add)
            cstore(low_ref, at, ((full[0] * factor).astype(BF16), (full[1] * factor).astype(BF16)))
            before = cload(h_ref, at, CHUNKS)
        rows = pl.ds(first, seg)
        leaving.append(copies.start(low_ref.at[rows], low_hbm.at[rows]))
    normed_here.wait()
    grad_b = dot_tn(normed_ref[...], low_ref[...])
    put_halves(grad_b, go_ref, send_ref)
    b_here.wait(), d_here.wait()
    prod = grad_b * b_ref[...].astype(F32)
    small_ref[...] = jnp.zeros_like(small_ref)
    n = gamma_ref.shape[1]
    small_ref[0:1, :n] = jnp.sum(sums[0], axis=0, keepdims=True)
    small_ref[0:1, n:] = jnp.sum(sums[1], axis=0, keepdims=True)
    small_ref[1:2, :] = jnp.sum(prod, axis=0, keepdims=True)
    small_ref[2:3, :] = jnp.sum(prod.T, axis=0, keepdims=True) + d_ref[...] * g_d_ref[...]
    small_ref[3:4, :] = g_d_ref[...]
    wait(leaving)


def input_kernel(
    gain_hbm, b_hbm, d_hbm, xs_hbm, cts_hbm, low_hbm, mixed_hbm,
    in_hbm, gain_ref, b_ref, d_ref, xs_ref, cts_ref, low_ref, mixed_ref, in_ref, sems,
):
    lanes, seg, width = in_ref.shape
    copies = Copies(sems)
    params = [copies.start(a, b) for a, b in ((gain_hbm, gain_ref), (b_hbm, b_ref), (d_hbm, d_ref))]
    here = copies.lanes(
        lanes, (low_hbm, low_ref), (mixed_hbm, mixed_ref), (xs_hbm, xs_ref), (cts_hbm, cts_ref)
    )
    wait(params)
    leaving = []
    order_back = scan_order(seg, True)
    for lane in range(lanes):
        rows = pl.ds(lane * seg, seg)
        wait(here[lane])
        grad_normed = dot_nt(low_ref[rows, :], b_ref[...]) + mixed_ref[rows, :] * d_ref[...]
        xhat, scale = norm_stats(xs_ref[rows, :].astype(F32))
        dxhat = grad_normed * gain_ref[...]
        one = jnp.mean(dxhat, axis=-1, keepdims=True)
        two = jnp.mean(dxhat * xhat, axis=-1, keepdims=True)
        grad = (cts_ref[rows, :].astype(F32) + (dxhat - one - xhat * two) * scale).astype(BF16)
        in_ref[lane] = dot_nn(order_back, grad).astype(BF16)
        leaving.append(copies.start(in_ref.at[lane], in_hbm.at[lane]))
    wait(leaving)


def finish_kernel(
    nu_hbm, th_hbm, gain_hbm, small_ref, pow_ref, gain_out, gamma_out, nu_out, th_out, d_out,
    nu_ref, th_ref, gain_ref, sems,
):
    n = nu_ref.shape[1]
    copies = Copies(sems)
    for copy in [copies.start(a, b) for a, b in ((nu_hbm, nu_ref), (th_hbm, th_ref), (gain_hbm, gain_ref))]:
        copy.wait()
    lam = cload(pow_ref, 0)
    p, q = small_ref[0:1, :n], small_ref[0:1, n:]
    nu_out[...] = -jnp.exp(nu_ref[...]) * (p * lam[0] + q * lam[1])
    th_out[...] = -jnp.exp(th_ref[...]) * (p * lam[1] - q * lam[0])
    gamma_out[...] = small_ref[1:2, :n] + small_ref[1:2, n:]
    gain_out[...] = small_ref[2:3, :] / gain_ref[...]
    d_out[...] = small_ref[3:4, :]


def swap(value, axis, bit):
    count = lax.axis_size(axis)
    return lax.ppermute(value, axis, [(i, i ^ (1 << bit)) for i in range(count)])


def entering(pair, backward, beside=None):
    lanes, n = pair.shape[0] // 2, pair.shape[1] // 2

    def mul(x, y):
        return jnp.concatenate(
            [x[:, :n] * y[:, :n] - x[:, n:] * y[:, n:], x[:, :n] * y[:, n:] + x[:, n:] * y[:, :n]], 1
        )

    count, mine = lax.axis_size("seq"), lax.axis_index("seq")
    total, decay = pair[:lanes], pair[lanes:]
    prefix = through = None
    for bit in range(count.bit_length() - 1):
        sent = jnp.concatenate([total, decay], 0)
        if beside is not None and bit == 1:
            sent, beside = tie(sent, beside)
        got = swap(sent, "seq", bit)
        other, other_decay = got[:lanes], got[lanes:]
        later = (lax.div(mine, 1 << bit) % 2 == 1) != backward
        if prefix is None:
            unit = jnp.concatenate([jnp.ones_like(pair[:lanes, :n]), jnp.zeros_like(pair[:lanes, n:])], 1)
            prefix = jnp.where(later, other, 0.0)
            through = jnp.where(later, other_decay, unit)
        else:
            prefix = jnp.where(later, prefix + mul(through, other), prefix)
            through = jnp.where(later, mul(through, other_decay), through)
        total = jnp.where(later, total + mul(decay, other), other + mul(other_decay, total))
        decay = mul(decay, other_decay)
    return prefix, beside


def bit_of(dim):
    axis, bit = dim
    return lax.axis_index(axis) // (1 << bit) % 2


def cut_rows(value, which):
    rows = value.shape[0] // 2
    return lax.dynamic_slice(value, (which * rows, 0), (rows, value.shape[1]))


def scatter(value, dim, extra=None):
    mine = bit_of(dim)
    send, keep = cut_rows(value, 1 - mine), cut_rows(value, mine)
    if extra is None:
        return keep + swap(send, *dim), None
    rows = send.shape[0]
    got = swap(jnp.concatenate([send, extra], 0), *dim)
    return keep + got[:rows], extra + got[rows:]


def gather(value, dim):
    mine, got = bit_of(dim), swap(value, *dim)
    return jnp.where(
        mine == 0, jnp.concatenate([value, got], 0), jnp.concatenate([got, value], 0)
    )


def bits(axis, first=0):
    return [(axis, bit) for bit in range(first, lax.axis_size(axis).bit_length() - 1)]


def tie(*values):
    return lax.optimization_barrier(values)


def dp_orders():
    return [bits("dp"), bits("dp")[::-1]]


def scatter_dp(parts, position, extra=None):
    orders = dp_orders()
    first, _ = scatter(parts[0], orders[0][position])
    second, extra = scatter(parts[1], orders[1][position], extra)
    return [first, second], extra


def gather_dp(parts, position):
    return [gather(part, order[position]) for part, order in zip(parts, dp_orders())]


def double(value, dim, extra=None):
    if extra is None:
        return value + swap(value, *dim), None
    rows = value.shape[0]
    both = jnp.concatenate([value, extra], 0)
    both = both + swap(both, *dim)
    return both[:rows], both[rows:]


def assemble_kernel(*refs):
    count = (len(refs) - 1) // 3
    mine, other, whole, sems = refs[:count], refs[count : 2 * count], refs[2 * count : -1], refs[-1]
    copies = Copies(sems)
    core = lax.rem(lax.axis_index("seq"), 2)
    for a, b, c in zip(mine, other, whole):
        rows = a.shape[0]
        first = pl.multiple_of(core * rows, rows)
        copies.start(a, c.at[pl.ds(first, rows)])
        copies.start(b, c.at[pl.ds(pl.multiple_of(rows - first, rows), rows)])
    for copy in copies.all:
        copy.wait()


def on_device(
    block_in, cotangent, bucket_id, assignment, norm_gain, b_proj, gamma_log, nu_log, theta_log,
    c_proj, d_skip, glu_weight,
):
    _, lanes, seg, width = block_in.shape
    n = nu_log.shape[0]
    two = 2 * n
    tokens = lanes * seg
    span = seg // CHUNKS
    short = seg * lax.axis_size("seq") // bucket_id.shape[2]
    gain, gamma, nu, theta, skip = (
        v.reshape(1, -1) for v in (norm_gain, gamma_log, nu_log, theta_log, d_skip)
    )
    hbm, vmem = pl.BlockSpec(memory_space=pltpu.HBM), pl.BlockSpec(memory_space=pltpu.VMEM)

    def call(kernel, name, micros, outs, far, near, fetched=None, scratch=(), sems=0, far_outs=0, limit=4, pin=False):
        fetched = far if fetched is None else fetched
        far = [pltpu.with_memory_space_constraint(v, pltpu.HBM) for v in far]
        if pin:
            near = [pltpu.with_memory_space_constraint(v, pltpu.VMEM) for v in near]
        shapes = [
            pltpu.HBM(shape, kind) if k < far_outs else jax.ShapeDtypeStruct(shape, kind)
            for k, (shape, kind) in enumerate(outs)
        ]
        room = [(pltpu.SMEM if v.dtype == jnp.int32 else pltpu.VMEM)(v.shape, v.dtype) for v in fetched]
        return pl.pallas_call(
            kernel,
            in_specs=[hbm] * len(far) + [vmem] * len(near),
            out_specs=[hbm] * far_outs + [vmem] * (len(outs) - far_outs),
            out_shape=shapes,
            scratch_shapes=room
            + [pltpu.VMEM(shape, kind) for shape, kind in scratch]
            + [pltpu.SemaphoreType.DMA((sems,))],
            compiler_params=pltpu.CompilerParams(vmem_limit_bytes=limit * 1024 * 1024),
            cost_estimate=cost(micros),
            name=name,
        )(*far, *near)

    low_rows, full_rows = ((tokens, width), BF16), ((tokens, two), F32)
    lane_rows = ((lanes, seg, width), BF16)
    xs, normed, loc, pair, powers, keep = call(
        functools.partial(first_kernel, short), "forward_local", 4,
        [
            low_rows, low_rows, full_rows, ((2 * lanes, two), F32), ((span, two), F32),
            ((lanes * CHUNKS, two), F32),
        ],
        [bucket_id[0], assignment, block_in[0], gain, b_proj, gamma, nu, theta], [],
        scratch=[low_rows, low_rows, full_rows], sems=4 * lanes + 7, far_outs=3, limit=12,
    )
    enter, _ = entering(pair, False)

    block_out, cts, h, carry, states, slope, pre, w_keep, w_send = call(
        block_kernel, "block", 7,
        [
            lane_rows, low_rows, full_rows, ((lanes * CHUNKS, two), F32), low_rows, full_rows,
            ((tokens, 2 * width), BF16), ((n, 2 * width), F32), ((n, 2 * width), F32),
        ],
        [cotangent[0], c_proj, skip, glu_weight, xs, normed, loc], [enter, powers, keep],
        scratch=[lane_rows, low_rows, low_rows], sems=7 * lanes + 3, far_outs=3, limit=20,
    )
    grad_mixed, adj, back_total, grad_d, c_keep, c_send = call(
        adjoint_kernel, "adjoint_local", 4,
        [
            full_rows, full_rows, ((lanes, two), F32), ((1, width), F32), ((n, width), F32),
            ((n, width), F32),
        ],
        [glu_weight, c_proj, normed], [pre, slope, states, powers, keep],
        scratch=[full_rows, full_rows, low_rows], sems=3 * lanes + 2, far_outs=2, limit=16,
    )

    decay = pair[lanes:]
    back_pair = jnp.concatenate(
        [back_total, jnp.concatenate([decay[:, :n], -decay[:, n:]], 1)], 0
    )
    w = w_keep + swap(w_send, "seq", 0)
    c = c_keep + swap(c_send, "seq", 0)
    wc = jnp.concatenate([w, c], 1)
    leave, wc = entering(back_pair, True, wc)
    half = wc.shape[1] // 2
    wc, _ = scatter_dp([wc[:, :half], wc[:, half:]], 0)

    back_low, b_keep, b_send, small = call(
        states_kernel, "adjoint_states", 3,
        [low_rows, ((n, two), F32), ((n, two), F32), ((8, two), F32)],
        [b_proj, gamma, skip, normed, h, adj], [leave, carry, powers, keep, grad_d],
        scratch=[low_rows, ((CHUNKS, two), F32)], sems=3 * lanes + 4, far_outs=1, limit=12,
    )

    b_send, *wc = tie(b_send, *wc)
    b = b_keep + swap(b_send, "seq", 0)
    small = small + swap(small, "seq", 0)
    b = [b[:, :n], b[:, n:]]
    small = small.reshape(-1, n)
    more = bits("seq", 1)
    steps = len(bits("dp"))
    for position in range(1, steps):
        wc, _ = scatter_dp(wc, position)
    for position in range(steps):
        b, small = scatter_dp(b, position, small)
    wc, b = jnp.concatenate(wc, 1), jnp.concatenate(b, 1)
    small = small.reshape(-1, two)
    for dim in more[:-1]:
        wc, _ = scatter(wc, dim)
        b, small = scatter(b, dim, small)
    wc, _ = double(wc, more[-1])
    b, small = double(b, more[-1], small)

    (grad_in,) = call(
        input_kernel, "back_input", 4, [lane_rows],
        [gain, b_proj, skip, xs, cts, back_low, grad_mixed], [],
        scratch=[lane_rows], sems=5 * lanes + 3, far_outs=1, limit=12,
    )
    finished = call(
        finish_kernel, "finish", 1, [((1, v), F32) for v in (width, n, n, n, width)],
        [nu, theta, gain], [small.reshape(8, two), powers], sems=3,
    )
    wc, b, grad_in, *finished = tie(wc, b, grad_in, *finished)
    grad_gain, grad_gamma, grad_nu, grad_theta, grad_d = finished

    for dim in more[:-1][::-1]:
        wc, b = gather(wc, dim), gather(b, dim)
    half = wc.shape[1] // 2
    wc, b = [wc[:, :half], wc[:, half:]], [b[:, :n], b[:, n:]]
    for position in reversed(range(steps)):
        wc, b = gather_dp(wc, position), gather_dp(b, position)
    wc, b = jnp.concatenate(wc, 1), jnp.concatenate(b, 1)
    mine = [wc[:, : 2 * width], wc[:, 2 * width :], b]
    other = [swap(v, "seq", 0) for v in mine]
    grad_w, grad_c, grad_b = call(
        assemble_kernel, "assemble", 2, [((2 * v.shape[0], v.shape[1]), F32) for v in mine],
        [], mine + other, sems=6, far_outs=3, pin=True,
    )
    return (
        block_out[None], grad_in[None], grad_gain[0], grad_b, grad_gamma[0], grad_nu[0], grad_theta[0],
        grad_c, grad_d[0], grad_w,
    )


def solution(mesh):
    rows = P("dp", None, "seq", None)
    in_specs = (rows, rows, P("dp", None, None), P("dp", None)) + (P(),) * 8
    out_specs = (rows, rows) + (P(),) * 8
    return jax.shard_map(
        on_device, mesh=mesh, in_specs=in_specs, out_specs=out_specs, check_vma=False
    )
```

```python
import functools

import jax
import jax.numpy as jnp
from jax import lax
from jax.experimental import pallas as pl
from jax.experimental.pallas import tpu as pltpu
from jax.sharding import PartitionSpec as P

EPS = 1e-05
CHUNKS = 8
LANE = 128
GELU_A = 0.044715
GELU_K = 0.7978845608028654
F32 = jnp.float32
BF16 = jnp.bfloat16


def dot_nt(left, right):
    return lax.dot_general(left, right, (((1,), (1,)), ((), ())), preferred_element_type=F32)


def dot_tn(left, right):
    return lax.dot_general(left, right, (((0,), (0,)), ((), ())), preferred_element_type=F32)


def dot_nn(left, right):
    return jnp.dot(left, right, preferred_element_type=F32)


def cmul(x, y):
    return x[0] * y[0] - x[1] * y[1], x[0] * y[1] + x[1] * y[0]


def cadd(x, y):
    return x[0] + y[0], x[1] + y[1]


def fma(a, x, y):
    return (y[0] - a[1] * x[1]) + a[0] * x[0], (y[1] + a[1] * x[0]) + a[0] * x[1]


def conj(x):
    return x[0], -x[1]


def cload(ref, first, count=1):
    n = ref.shape[-1] // 2
    return ref[first : first + count, :n], ref[first : first + count, n:]


def cstore(ref, first, value):
    n = ref.shape[-1] // 2
    rows = value[0].shape[0]
    ref[first : first + rows, :n], ref[first : first + rows, n:] = value


def kept(ref, row, value):
    keep = cload(ref, row)
    return value[0] * keep[0], value[1] * keep[1]


def scan_order(seg, back=False):
    row = lax.broadcasted_iota(jnp.int32, (seg, seg), 0)
    column = lax.broadcasted_iota(jnp.int32, (seg, seg), 1)
    if back:
        row, column = column, row
    span = seg // CHUNKS
    hit = (row % CHUNKS == column // span) & (row // CHUNKS == column % span)
    return jnp.where(hit, 1.0, 0.0).astype(BF16)


def fill_keeps(bucket, assign, keep_ref, lanes, seg, short):
    own = lax.axis_index("seq")
    for lane in range(lanes):
        pattern = assign[0, lane]
        for chunk in range(CHUNKS):
            token = own * seg + chunk * (seg // CHUNKS)
            here = bucket[pattern, lax.div(token, short)]
            span = jnp.where(here == 0, short, jnp.where(here == 1, 4 * short, 16 * short))
            keep = jnp.where(lax.rem(token, span) == 0, 0.0, 1.0).astype(F32)
            row = lane * CHUNKS + chunk
            keep_ref[row : row + 1, :] = jnp.full((1, keep_ref.shape[1]), keep)


def norm_stats(rows):
    mean = jnp.mean(rows, axis=-1, keepdims=True)
    centred = rows - mean
    var = jnp.mean(centred * centred, axis=-1, keepdims=True)
    scale = lax.rsqrt(var + EPS)
    return centred * scale, scale


def cost(micros):
    return pl.CostEstimate(flops=int(micros * 1.1e9), bytes_accessed=int(micros * 3e6), transcendentals=0)


def put_halves(value, keep, send):
    rows = value.shape[0] // 2
    first = lax.rem(lax.axis_index("seq"), 2) == 0
    top, bottom = value[:rows], value[rows:]
    keep[...] = jnp.where(first, top, bottom)
    send[...] = jnp.where(first, bottom, top)


class Copies:
    def __init__(self, sems):
        self.sems, self.all = sems, []

    def start(self, source, target):
        copy = pltpu.make_async_copy(source, target, self.sems.at[len(self.all)])
        copy.start()
        self.all.append(copy)
        return copy

    def lanes(self, lanes, *pairs):
        return [
            [self.start(lane_of(source, lane, lanes), lane_of(target, lane, lanes)) for source, target in pairs]
            for lane in range(lanes)
        ]


def lane_of(ref, lane, lanes):
    if len(ref.shape) == 3:
        return ref.at[lane]
    rows = ref.shape[0] // lanes
    return ref.at[pl.ds(lane * rows, rows)]


def wait(copies):
    for copy in copies:
        copy.wait()


def first_kernel(
    short, bucket_hbm, assign_hbm, x_hbm, gain_hbm, b_hbm, gamma_hbm, nu_hbm, th_hbm,
    xs_hbm, normed_hbm, loc_hbm, pair_ref, pow_ref, keep_ref,
    bucket, assign, x_ref, gain_ref, b_ref, gamma_ref, nu_ref, th_ref, xs_ref, normed_ref, loc_ref, sems,
):
    lanes, seg, width = x_ref.shape
    span = seg // CHUNKS
    copies = Copies(sems)
    x_here = copies.lanes(lanes, (x_hbm, x_ref))
    nu_here, th_here = copies.start(nu_hbm, nu_ref), copies.start(th_hbm, th_ref)
    gain_here, gamma_here = copies.start(gain_hbm, gain_ref), copies.start(gamma_hbm, gamma_ref)
    b_here = copies.start(b_hbm, b_ref)
    tables = copies.start(bucket_hbm, bucket), copies.start(assign_hbm, assign)
    leaving = []

    order = scan_order(seg)
    nu_here.wait(), th_here.wait()
    modulus = jnp.exp(-jnp.exp(nu_ref[...]))
    phase = jnp.exp(th_ref[...])
    cstore(pow_ref, 0, (modulus * jnp.cos(phase), modulus * jnp.sin(phase)))
    size = 1
    while size < span:
        cstore(pow_ref, size, cmul(cload(pow_ref, 0, size), cload(pow_ref, size - 1)))
        size *= 2

    gain_here.wait(), gamma_here.wait()
    lam = cload(pow_ref, 0)
    lam_span = cload(pow_ref, span - 1)
    ends = []
    factor = jnp.exp(gamma_ref[...])
    factor = jnp.concatenate([factor, factor], 1)
    for lane in range(lanes):
        rows = pl.ds(lane * seg, seg)
        wait(x_here[lane])
        x = dot_nn(order, x_ref[lane])
        xs_ref[rows, :] = x.astype(BF16)
        xhat, _ = norm_stats(x)
        low = (xhat * gain_ref[...]).astype(BF16)
        normed_ref[rows, :] = low
        if lane == 0:
            b_here.wait()
        loc_ref[rows, :] = dot_nn(low, b_ref[...]) * factor
        for source, target in ((xs_ref, xs_hbm), (normed_ref, normed_hbm)):
            leaving.append(copies.start(source.at[rows], target.at[rows]))
        h = cload(loc_ref, lane * seg, CHUNKS)
        for step in range(1, span):
            at = lane * seg + step * CHUNKS
            h = fma(lam, h, cload(loc_ref, at, CHUNKS))
            cstore(loc_ref, at, h)
        leaving.append(copies.start(loc_ref.at[rows], loc_hbm.at[rows]))
        ends.append(h)

    wait(tables)
    fill_keeps(bucket, assign, keep_ref, lanes, seg, short)
    for lane, h in enumerate(ends):
        state = h[0][0:1], h[1][0:1]
        decay = kept(keep_ref, lane * CHUNKS, lam_span)
        for chunk in range(1, CHUNKS):
            step = kept(keep_ref, lane * CHUNKS + chunk, lam_span)
            state = fma(step, state, (h[0][chunk : chunk + 1], h[1][chunk : chunk + 1]))
            decay = cmul(step, decay)
        cstore(pair_ref, lane, state)
        cstore(pair_ref, lanes + lane, decay)
    wait(leaving)


def order_kernel(ct_hbm, cts_hbm, ct_ref, cts_ref, sems):
    lanes, seg, _ = ct_ref.shape
    copies = Copies(sems)
    here = copies.lanes(lanes, (ct_hbm, ct_ref))
    order = scan_order(seg)
    leaving = []
    for lane in range(lanes):
        rows = pl.ds(lane * seg, seg)
        wait(here[lane])
        cts_ref[rows, :] = dot_nn(order, ct_ref[lane]).astype(BF16)
        leaving.append(copies.start(cts_ref.at[rows], cts_hbm.at[rows]))
    wait(leaving)


def block_kernel(
    w_hbm, c_hbm, d_hbm, xs_hbm, normed_hbm, loc_hbm, cts_hbm, enter_ref, pow_ref, keep_ref,
    out_hbm, h_hbm, mixed_hbm, adj_hbm, carry_hbm, c_go_hbm, back_ref, g_d_ref, w_go_ref, w_send_ref, c_send_ref,
    carry_ref, c_go_ref, w_ref, c_ref, d_ref, xs_ref, normed_ref, h_ref, cts_ref,
    out_ref, states_ref, gelu_ref, pre_ref, slope_ref, mixed_ref, low_ref, adj_ref, sems,
):
    lanes, width = enter_ref.shape[0], d_ref.shape[1]
    seg = h_ref.shape[0] // lanes
    span = seg // CHUNKS
    copies = Copies(sems)
    one, rest = pl.ds(0, seg), pl.ds(seg, (lanes - 1) * seg)
    arrays = (loc_hbm, h_ref), (normed_hbm, normed_ref), (xs_hbm, xs_ref), (cts_hbm, cts_ref)
    loc_here = copies.start(loc_hbm.at[one], h_ref.at[one])
    c_here, d_here = copies.start(c_hbm, c_ref), copies.start(d_hbm, d_ref)
    normed_here = copies.start(normed_hbm.at[one], normed_ref.at[one])
    w_here = copies.start(w_hbm, w_ref)
    late_here = [copies.start(a.at[one], b.at[one]) for a, b in arrays[2:]]
    rest_here = [copies.start(a.at[rest], b.at[rest]) for a, b in arrays]
    leaving = []
    lam_span = cload(pow_ref, span - 1)
    for lane in range(lanes):
        first = lane * seg
        rows = pl.ds(first, seg)
        if lane == 0:
            loc_here.wait()
        elif lane == 1:
            wait(rest_here)
        last = first + (span - 1) * CHUNKS
        state = kept(keep_ref, lane * CHUNKS, cload(enter_ref, lane))
        cstore(carry_ref, lane * CHUNKS, state)
        for chunk in range(1, CHUNKS):
            state = fma(lam_span, state, cload(h_ref, last + chunk - 1))
            state = kept(keep_ref, lane * CHUNKS + chunk, state)
            cstore(carry_ref, lane * CHUNKS + chunk, state)
        carry = cload(carry_ref, lane * CHUNKS, CHUNKS)
        for step in range(span):
            at = first + step * CHUNKS
            cstore(h_ref, at, fma(cload(pow_ref, step), carry, cload(h_ref, at, CHUNKS)))
        leaving.append(copies.start(h_ref.at[rows], h_hbm.at[rows]))

        states = h_ref[rows, :].astype(BF16)
        states_ref[rows, :] = states
        if lane == 0:
            wait([normed_here, c_here, d_here])
        mixed = dot_nn(states, c_ref[...]) + d_ref[...] * normed_ref[rows, :].astype(F32)
        square = mixed * mixed
        tanh = jnp.tanh(GELU_K * mixed * (1.0 + GELU_A * square))
        half_up = 0.5 * (1.0 + tanh)
        gelu = (mixed * half_up).astype(BF16)
        gelu_ref[rows, :] = gelu
        slope_ref[rows, :] = half_up + 0.5 * GELU_K * mixed * (1.0 - tanh * tanh) * (
            1.0 + 3.0 * GELU_A * square
        )
        if lane == 0:
            w_here.wait()
        pre = dot_nn(gelu, w_ref[...])
        value = pre[:, :width]
        sig = jax.nn.sigmoid(pre[:, width:])
        gated = value * sig
        if lane == 0:
            wait(late_here)
        out_ref[rows, :] = (xs_ref[rows, :].astype(F32) + gated).astype(BF16)
        leaving.append(copies.start(out_ref.at[rows], out_hbm.at[rows]))
        grad_value = cts_ref[rows, :].astype(F32) * sig
        pre_ref[rows, :width] = grad_value.astype(BF16)
        pre_ref[rows, width:] = (grad_value * (value - gated)).astype(BF16)

    lam, lam_span = conj(cload(pow_ref, 0)), conj(lam_span)
    total = None
    for lane in range(lanes):
        rows = pl.ds(lane * seg, seg)
        grad_mixed = dot_nt(pre_ref[rows, :], w_ref[...]) * slope_ref[rows, :]
        mixed_ref[rows, :] = grad_mixed
        leaving.append(copies.start(mixed_ref.at[rows], mixed_hbm.at[rows]))
        add = jnp.sum(grad_mixed * normed_ref[rows, :].astype(F32), axis=0, keepdims=True)
        total = add if total is None else total + add
        low = grad_mixed.astype(BF16)
        low_ref[rows, :] = low
        adj_ref[rows, :] = dot_nt(low, c_ref[...])
        adj = cload(adj_ref, (lane + 1) * seg - CHUNKS, CHUNKS)
        for step in reversed(range(span - 1)):
            at = lane * seg + step * CHUNKS
            adj = fma(lam, adj, cload(adj_ref, at, CHUNKS))
            cstore(adj_ref, at, adj)
        leaving.append(copies.start(adj_ref.at[rows], adj_hbm.at[rows]))
        state = None
        for chunk in reversed(range(CHUNKS)):
            here = adj[0][chunk : chunk + 1], adj[1][chunk : chunk + 1]
            state = here if state is None else fma(lam_span, state, here)
            state = kept(keep_ref, lane * CHUNKS + chunk, state)
        cstore(back_ref, lane, state)
    g_d_ref[...] = total
    leaving.append(copies.start(carry_ref, carry_hbm))
    put_halves(dot_tn(states_ref[...], low_ref[...]), c_go_ref, c_send_ref)
    leaving.append(copies.start(c_go_ref, c_go_hbm))
    put_halves(dot_tn(gelu_ref[...], pre_ref[...]), w_go_ref, w_send_ref)
    wait(leaving)


def states_kernel(
    c_go_hbm, carry_ref, b_ref, gamma_ref, d_ref, normed_ref, h_ref, adj_ref, leave_ref, pow_ref, keep_ref, g_d_ref,
    c_got_ref,
    low_hbm, go_ref, send_ref, c_ref, low_ref, after_ref, small_ref, sems,
):
    copies = Copies(sems)
    c_here = copies.start(c_go_hbm, c_ref)
    leaving = []
    lanes = leave_ref.shape[0]
    seg = normed_ref.shape[0] // lanes
    span = seg // CHUNKS
    back = conj(cload(pow_ref, span - 1))
    factor = jnp.exp(gamma_ref[...])
    sums = None
    for lane in range(lanes):
        first = lane * seg
        state = cload(leave_ref, lane)
        cstore(after_ref, CHUNKS - 1, state)
        for chunk in reversed(range(1, CHUNKS)):
            state = fma(back, state, cload(adj_ref, first + chunk))
            state = kept(keep_ref, lane * CHUNKS + chunk, state)
            cstore(after_ref, chunk - 1, state)
        after = cload(after_ref, 0, CHUNKS)
        before = cload(carry_ref, lane * CHUNKS, CHUNKS)
        for step in range(span):
            at = first + step * CHUNKS
            full = fma(conj(cload(pow_ref, span - 1 - step)), after, cload(adj_ref, at, CHUNKS))
            add = cmul(conj(before), full)
            sums = add if sums is None else cadd(sums, add)
            cstore(low_ref, at, ((full[0] * factor).astype(BF16), (full[1] * factor).astype(BF16)))
            before = cload(h_ref, at, CHUNKS)
        rows = pl.ds(first, seg)
        leaving.append(copies.start(low_ref.at[rows], low_hbm.at[rows]))
    grad_b = dot_tn(normed_ref[...], low_ref[...])
    n = gamma_ref.shape[1]
    prod = grad_b * b_ref[...].astype(F32)
    small_ref[...] = jnp.zeros_like(small_ref)
    small_ref[0:1, :n] = jnp.sum(sums[0], axis=0, keepdims=True)
    small_ref[0:1, n:] = jnp.sum(sums[1], axis=0, keepdims=True)
    small_ref[1:2, :] = jnp.sum(prod, axis=0, keepdims=True)
    small_ref[8:9, :] = jnp.sum(prod.T, axis=0, keepdims=True) + d_ref[...] * g_d_ref[...]
    small_ref[9:10, :] = g_d_ref[...]
    put_halves(grad_b, go_ref.at[pl.ds(0, n)], send_ref.at[pl.ds(0, n)])
    put_halves(small_ref[...], go_ref.at[pl.ds(n, 8)], send_ref.at[pl.ds(n, 8)])
    c_here.wait()
    c_ref[...] += c_got_ref[...]
    wait(leaving)


def pieces_kernel(c_ref, b_keep_ref, b_got_ref, own_ref, small_ref, *send_refs):
    count, n = len(send_refs) + 1, c_ref.shape[0]
    rows = n // count
    mine = lax.axis_index("dp")
    small = b_keep_ref[n:, :] + b_got_ref[n:, :]
    small_ref[...] = small
    for mask in range(count):
        start = pl.multiple_of((mine ^ mask) * rows, rows)
        at = pl.ds(start, rows)
        c = c_ref[at, :]
        b = b_keep_ref[at, :] + b_got_ref[at, :]
        if mask == 0:
            own_ref[0], own_ref[1] = c, b
        else:
            ref = send_refs[mask - 1]
            ref[:rows, :], ref[rows : 2 * rows, :], ref[2 * rows :, :] = c, b, small


def input_kernel(
    gain_hbm, b_hbm, d_hbm, xs_hbm, cts_hbm, low_hbm, mixed_hbm, out_hbm,
    in_hbm, block_hbm, gain_ref, b_ref, d_ref, xs_ref, cts_ref, low_ref, mixed_ref, out_ref,
    in_ref, block_ref, sems,
):
    lanes, seg, width = in_ref.shape
    copies = Copies(sems)
    params = [copies.start(a, b) for a, b in ((gain_hbm, gain_ref), (b_hbm, b_ref), (d_hbm, d_ref))]
    here = copies.lanes(
        lanes, (low_hbm, low_ref), (mixed_hbm, mixed_ref), (xs_hbm, xs_ref), (cts_hbm, cts_ref),
        (out_hbm, out_ref),
    )
    wait(params)
    leaving = []
    order_back = scan_order(seg, True)
    for lane in range(lanes):
        rows = pl.ds(lane * seg, seg)
        wait(here[lane])
        grad_normed = dot_nt(low_ref[rows, :], b_ref[...]) + mixed_ref[rows, :] * d_ref[...]
        xhat, scale = norm_stats(xs_ref[rows, :].astype(F32))
        dxhat = grad_normed * gain_ref[...]
        one = jnp.mean(dxhat, axis=-1, keepdims=True)
        two = jnp.mean(dxhat * xhat, axis=-1, keepdims=True)
        grad = (cts_ref[rows, :].astype(F32) + (dxhat - one - xhat * two) * scale).astype(BF16)
        in_ref[lane] = dot_nn(order_back, grad).astype(BF16)
        leaving.append(copies.start(in_ref.at[lane], in_hbm.at[lane]))
        block_ref[lane] = dot_nn(order_back, out_ref[rows, :]).astype(BF16)
        leaving.append(copies.start(block_ref.at[lane], block_hbm.at[lane]))
    wait(leaving)


def finish_kernel(
    nu_hbm, th_hbm, gain_hbm, small_ref, pow_ref, gain_out, gamma_out, nu_out, th_out, d_out,
    nu_ref, th_ref, gain_ref, sems,
):
    n = nu_ref.shape[1]
    copies = Copies(sems)
    for copy in [copies.start(a, b) for a, b in ((nu_hbm, nu_ref), (th_hbm, th_ref), (gain_hbm, gain_ref))]:
        copy.wait()
    lam = cload(pow_ref, 0)
    p, q = small_ref[0:1, :n], small_ref[0:1, n:]
    nu_out[...] = -jnp.exp(nu_ref[...]) * (p * lam[0] + q * lam[1])
    th_out[...] = -jnp.exp(th_ref[...]) * (p * lam[1] - q * lam[0])
    gamma_out[...] = small_ref[1:2, :n] + small_ref[1:2, n:]
    gain_out[...] = small_ref[8:9, :] / gain_ref[...]
    d_out[...] = small_ref[9:10, :]


def swap(value, axis, bit):
    count = lax.axis_size(axis)
    return lax.ppermute(value, axis, [(i, i ^ (1 << bit)) for i in range(count)])


def entering(pair, backward, beside=None):
    lanes, n = pair.shape[0] // 2, pair.shape[1] // 2

    def mul(x, y):
        return jnp.concatenate(
            [x[:, :n] * y[:, :n] - x[:, n:] * y[:, n:], x[:, :n] * y[:, n:] + x[:, n:] * y[:, :n]], 1
        )

    def join(early, late):
        return late[0] + mul(late[1], early[0]), mul(late[1], early[1])

    count, mine = lax.axis_size("seq"), lax.axis_index("seq")
    one = jnp.concatenate([jnp.ones_like(pair[:lanes, :n]), jnp.zeros_like(pair[:lanes, n:])], 1)
    before = jnp.zeros_like(one), one
    bit = 0
    while 1 << bit < count:
        size = 2 if bit == 0 else min(4, count >> bit)
        if beside is not None and bit == (1 if not backward else 0):
            pair, beside = tie(pair, beside)
        parts = [pair] + [
            lax.ppermute(pair, "seq", [(i, i ^ (mask << bit)) for i in range(count)])
            for mask in reversed(range(1, size))
        ][::-1]
        place = mine // (1 << bit) % size ^ (size - 1 if backward else 0)
        ordered = []
        for k in range(size):
            part = parts[0]
            for mask in range(1, size):
                part = jnp.where(place ^ k == mask, parts[mask], part)
            ordered.append((part[:lanes], part[lanes:]))
        sofar = None
        for k, item in enumerate(ordered):
            if k:
                joined = join(sofar, before)
                before = tuple(jnp.where(place == k, new, old) for new, old in zip(joined, before))
            sofar = item if sofar is None else join(sofar, item)
        pair = jnp.concatenate(sofar, 0)
        bit += size.bit_length() - 1
    return before[0] if beside is None else (before[0], beside)


def bits(axis, first=0):
    return [(axis, bit) for bit in range(first, lax.axis_size(axis).bit_length() - 1)]


def phases():
    return [bits("dp") + bits("seq", 1), bits("dp")[::-1] + bits("seq", 1)[::-1]]


def hop(value, phase):
    orders, count = phases(), lax.axis_size("seq")
    pairs = []
    for device in range(lax.axis_size("dp") * count):
        axis, bit = orders[device % 2][phase]
        pairs.append((device, device ^ ((1 << bit) * (count if axis == "dp" else 1))))
    return lax.ppermute(value, ("dp", "seq"), pairs)


def my_bit(phase):
    one, two = (lax.axis_index(axis) // (1 << bit) % 2 for axis, bit in (o[phase] for o in phases()))
    return jnp.where(lax.axis_index("seq") % 2 == 0, one, two)


def piece(value, which, count):
    rows = value.shape[1] // count
    return lax.dynamic_slice(value, (0, which * rows, 0), (value.shape[0], rows, value.shape[2]))


def pack(value, extra):
    if extra is None:
        return value
    return jnp.concatenate([value.reshape(-1, value.shape[2]), extra], 0)


def unpack(sent, value, extra):
    if extra is None:
        return sent, None
    rows = value.shape[0] * value.shape[1]
    return sent[:rows].reshape(value.shape), sent[rows:]


def tree_sum(values):
    while len(values) > 1:
        values = [a + b for a, b in zip(values[::2], values[1::2])]
    return values[0]


def scatter(value, phase, extra=None):
    mine = my_bit(phase)
    send, keep = piece(value, 1 - mine, 2), piece(value, mine, 2)
    got, more = unpack(hop(pack(send, extra), phase), send, extra)
    return keep + got, None if extra is None else extra + more


def double(value, phase, extra=None):
    got, more = unpack(hop(pack(value, extra), phase), value, extra)
    return value + got, None if extra is None else extra + more


def gather(value, phase):
    got = hop(value, phase)
    return join_rows([value, got], my_bit(phase))


def join_rows(parts, mine):
    count = len(parts)
    if count == 1:
        return parts[0]
    half = count // 2
    low = join_rows(parts[:half], mine % half)
    high = join_rows(parts[half:], mine % half)
    first = mine // half == 0
    return jnp.where(first, jnp.concatenate([low, high], 1), jnp.concatenate([high, low], 1))


def across(value, mask):
    return lax.ppermute(value, "dp", [(i, i ^ mask) for i in range(lax.axis_size("dp"))])


def sum_dp(own, sends, extra):
    parts, extras = [own], [extra]
    for mask, send in enumerate(sends):
        got, more = unpack(across(send, mask + 1), own, extra)
        parts.append(got)
        extras.append(more)
    return tree_sum(parts), tree_sum(extras)


def gather_dp(value):
    count, mine = lax.axis_size("dp"), lax.axis_index("dp")
    parts = [value]
    for mask in reversed(range(1, count)):
        parts.insert(1, across(value, mask))
    return join_rows(parts, mine)


def tie(*values):
    return lax.optimization_barrier(values)


def after(value, *others):
    for other in others:
        value = value + jnp.minimum(jnp.abs(other[(0,) * other.ndim]), 0.0)
    return value


def assemble_kernel(mine, other, *refs):
    whole, sems = refs[:-1], refs[-1]
    copies = Copies(sems)
    rows = mine.shape[0]
    first = pl.multiple_of(lax.rem(lax.axis_index("seq"), 2) * rows, rows)
    column = 0
    for out in whole:
        columns = pl.ds(column, out.shape[1])
        copies.start(mine.at[:, columns], out.at[pl.ds(first, rows)])
        copies.start(other.at[:, columns], out.at[pl.ds(pl.multiple_of(rows - first, rows), rows)])
        column += out.shape[1]
    wait(copies.all)


def on_device(
    block_in, cotangent, bucket_id, assignment, norm_gain, b_proj, gamma_log, nu_log, theta_log,
    c_proj, d_skip, glu_weight,
):
    _, lanes, seg, width = block_in.shape
    n = nu_log.shape[0]
    two = 2 * n
    tokens = lanes * seg
    span = seg // CHUNKS
    short = seg * lax.axis_size("seq") // bucket_id.shape[2]
    gain, gamma, nu, theta, skip = (
        v.reshape(1, -1) for v in (norm_gain, gamma_log, nu_log, theta_log, d_skip)
    )
    hbm, vmem = pl.BlockSpec(memory_space=pltpu.HBM), pl.BlockSpec(memory_space=pltpu.VMEM)

    def call(kernel, name, micros, outs, far, near, fetched=None, scratch=(), sems=0, far_outs=0, limit=4, pin=False, wait_for=()):
        fetched = far if fetched is None else fetched
        far = [pltpu.with_memory_space_constraint(v, pltpu.HBM) for v in far]
        if pin:
            near = [pltpu.with_memory_space_constraint(v, pltpu.VMEM) for v in near]
        shapes = [
            pltpu.HBM(shape, kind) if k < far_outs else jax.ShapeDtypeStruct(shape, kind)
            for k, (shape, kind) in enumerate(outs)
        ]
        room = [(pltpu.SMEM if v.dtype == jnp.int32 else pltpu.VMEM)(v.shape, v.dtype) for v in fetched]
        count, extra = len(far) + len(near), len(wait_for)

        def body(*refs):
            kernel(*refs[:count], *refs[count + extra :])

        return pl.pallas_call(
            body,
            in_specs=[hbm] * len(far) + [vmem] * len(near) + [pl.BlockSpec(memory_space=pl.ANY)] * extra,
            out_specs=[hbm] * far_outs + [vmem] * (len(outs) - far_outs),
            out_shape=shapes,
            scratch_shapes=room
            + [pltpu.VMEM(shape, kind) for shape, kind in scratch]
            + ([pltpu.SemaphoreType.DMA((sems,))] if sems else []),
            compiler_params=pltpu.CompilerParams(vmem_limit_bytes=limit * 1024 * 1024),
            cost_estimate=cost(micros),
            name=name,
        )(*far, *near, *wait_for)

    low_rows, full_rows = ((tokens, width), BF16), ((tokens, two), F32)
    lane_rows = ((lanes, seg, width), BF16)
    xs, normed, loc, pair, powers, keep = call(
        functools.partial(first_kernel, short), "forward_local", 4,
        [
            low_rows, low_rows, full_rows, ((2 * lanes, two), F32), ((span, two), F32),
            ((lanes * CHUNKS, two), F32),
        ],
        [bucket_id[0], assignment, block_in[0], gain, b_proj, gamma, nu, theta], [],
        scratch=[low_rows, low_rows, full_rows], sems=4 * lanes + 7, far_outs=3, limit=12,
    )
    enter, cotangent_later = entering(pair, False, cotangent[0])
    (cts,) = call(
        order_kernel, "cotangent_order", 2, [low_rows], [cotangent_later], [],
        scratch=[low_rows], sems=2 * lanes, far_outs=1, limit=8,
    )

    chunk_rows, half_rows = ((lanes * CHUNKS, two), F32), ((n, width), F32)
    out, h, grad_mixed, adj, carry, c_keep, back_total, grad_d, w_keep, w_send, c_send = call(
        block_kernel, "block", 10,
        [
            low_rows, full_rows, full_rows, full_rows, chunk_rows, half_rows, ((lanes, two), F32),
            ((1, width), F32), ((n, 2 * width), F32), ((n, 2 * width), F32), half_rows,
        ],
        [glu_weight, c_proj, skip, xs, normed, loc, cts], [enter, powers, keep], fetched=(),
        scratch=[
            chunk_rows, half_rows, ((width, 2 * width), BF16), ((two, width), BF16), ((1, width), F32),
            low_rows, low_rows, full_rows, low_rows,
            low_rows, low_rows, low_rows, ((tokens, 2 * width), BF16), full_rows, full_rows, low_rows,
            full_rows,
        ],
        sems=4 * lanes + 13, far_outs=6, limit=36,
    )

    decay = pair[lanes:]
    back_pair = jnp.concatenate(
        [back_total, jnp.concatenate([decay[:, :n], -decay[:, n:]], 1)], 0
    )
    near, last = len(bits("dp")), len(phases()[0]) - 1
    c_got = swap(c_send, "seq", 0)
    w = (w_keep + swap(w_send, "seq", 0))[None]
    leave, w = entering(back_pair, True, w)
    w, _ = scatter(w, 0)

    back_low, b_keep, b_send, c = call(
        states_kernel, "adjoint_states", 3,
        [low_rows, ((n + 8, two), F32), ((n + 8, two), F32), half_rows],
        [c_keep], [carry, b_proj, gamma, skip, normed, h, adj, leave, powers, keep, grad_d, c_got], fetched=(),
        scratch=[low_rows, ((CHUNKS, two), F32), ((16, two), F32)],
        sems=lanes + 1, far_outs=1, limit=8, wait_for=[w],
    )

    def back_input(back_low):
        return call(
            input_kernel, "back_input", 4, [lane_rows, lane_rows],
            [gain, b_proj, skip, xs, cts, back_low, grad_mixed, out], [], wait_for=[cb, finished[0], w],
            scratch=[lane_rows, lane_rows], sems=7 * lanes + 3, far_outs=2, limit=12,
        )

    for phase in range(1, near):
        w, _ = scatter(w, phase)
    groups = lax.axis_size("dp")
    cut = n // groups
    own, small, *sends = call(
        pieces_kernel, "pieces", 1,
        [((2, cut, width), F32), ((8, two), F32)] + [((2 * cut + 8, width), F32)] * (groups - 1),
        [], [c, b_keep, swap(b_send, "seq", 0)], wait_for=[w] if True else [],
    )
    cb, small = sum_dp(own, sends, small)

    def only(step):
        return lambda value, extra=None: (step(value), extra)

    steps = [functools.partial(scatter, phase=p) for p in range(near, last)]
    steps += [functools.partial(double, phase=last)]
    steps += [only(functools.partial(gather, phase=p)) for p in reversed(range(near, last))]
    ahead = steps + [only(functools.partial(gather, phase=p)) for p in reversed(range(near))]
    lead = 1
    for turn in range(lead):
        w, _ = ahead[turn](w)
    for turn, step in enumerate(steps):
        if turn + lead < len(ahead):
            w_next, _ = ahead[turn + lead](w)
        cb, small = step(cb, extra=small)
        w = w_next
    for turn in range(len(steps) + lead, len(ahead)):
        w, _ = ahead[turn](w)
    got = swap(small, "seq", 0)
    small = join_rows([small[None], got[None]], lax.axis_index("seq") % 2)[0]
    finished = call(
        finish_kernel, "finish", 1, [((1, v), F32) for v in (width, n, n, n, width)],
        [nu, theta, gain], [small, powers], sems=3,
    )
    grad_in, block_out = back_input(back_low)
    cb = gather_dp(cb)
    cb, grad_in, block_out = tie(cb, grad_in, block_out)
    w, cb = w[0], jnp.concatenate([cb[0], cb[1]], 1)

    grad_gain, grad_gamma, grad_nu, grad_theta, grad_d = finished

    def assemble(mine, widths, wait_for):
        return call(
            assemble_kernel, "assemble", 2, [((2 * mine.shape[0], v), F32) for v in widths],
            [], [mine, swap(mine, "seq", 0)], sems=2 * len(widths), far_outs=len(widths), pin=True, wait_for=wait_for,
        )

    (grad_w,) = assemble(w, [2 * width], [grad_in])
    grad_c, grad_b = assemble(cb, [width, two], [])
    return (
        block_out[None], grad_in[None], grad_gain[0], grad_b, grad_gamma[0], grad_nu[0], grad_theta[0],
        grad_c, grad_d[0], grad_w,
    )


def solution(mesh):
    rows = P("dp", None, "seq", None)
    in_specs = (rows, rows, P("dp", None, None), P("dp", None)) + (P(),) * 8
    out_specs = (rows, rows) + (P(),) * 8
    return jax.shard_map(
        on_device, mesh=mesh, in_specs=in_specs, out_specs=out_specs, check_vma=False
    )
```

```python
import functools

import jax
import jax.numpy as jnp
from jax import lax
from jax.experimental import pallas as pl
from jax.experimental.pallas import tpu as pltpu
from jax.sharding import PartitionSpec as P

EPS = 1e-05
CHUNKS = 8
GELU_A = 0.044715
GELU_K = 0.7978845608028654
F32 = jnp.float32
BF16 = jnp.bfloat16


def dot_nt(left, right):
    return lax.dot_general(left, right, (((1,), (1,)), ((), ())), preferred_element_type=F32)


def dot_tn(left, right):
    return lax.dot_general(left, right, (((0,), (0,)), ((), ())), preferred_element_type=F32)


def dot_nn(left, right):
    return jnp.dot(left, right, preferred_element_type=F32)


def cmul(x, y):
    return x[0] * y[0] - x[1] * y[1], x[0] * y[1] + x[1] * y[0]


def cadd(x, y):
    return x[0] + y[0], x[1] + y[1]


def fma(a, x, y):
    return (y[0] - a[1] * x[1]) + a[0] * x[0], (y[1] + a[1] * x[0]) + a[0] * x[1]


def conj(x):
    return x[0], -x[1]


def cload(ref, first, count=1):
    n = ref.shape[-1] // 2
    return ref[first : first + count, :n], ref[first : first + count, n:]


def cstore(ref, first, value):
    n = ref.shape[-1] // 2
    rows = value[0].shape[0]
    ref[first : first + rows, :n], ref[first : first + rows, n:] = value


def kept(ref, row, value):
    keep = cload(ref, row)
    return value[0] * keep[0], value[1] * keep[1]


def scan_order(seg, back=False):
    row = lax.broadcasted_iota(jnp.int32, (seg, seg), 0)
    column = lax.broadcasted_iota(jnp.int32, (seg, seg), 1)
    if back:
        row, column = column, row
    span = seg // CHUNKS
    hit = (row % CHUNKS == column // span) & (row // CHUNKS == column % span)
    return jnp.where(hit, 1.0, 0.0).astype(BF16)


def fill_keeps(bucket, assign, keep_ref, lanes, seg, short):
    own = lax.axis_index("seq")
    for lane in range(lanes):
        pattern = assign[0, lane]
        for chunk in range(CHUNKS):
            token = own * seg + chunk * (seg // CHUNKS)
            here = bucket[pattern, lax.div(token, short)]
            span = jnp.where(here == 0, short, jnp.where(here == 1, 4 * short, 16 * short))
            keep = jnp.where(lax.rem(token, span) == 0, 0.0, 1.0).astype(F32)
            row = lane * CHUNKS + chunk
            keep_ref[row : row + 1, :] = jnp.full((1, keep_ref.shape[1]), keep)


def norm_stats(rows):
    mean = jnp.mean(rows, axis=-1, keepdims=True)
    centred = rows - mean
    var = jnp.mean(centred * centred, axis=-1, keepdims=True)
    scale = lax.rsqrt(var + EPS)
    return centred * scale, scale


def cost(micros):
    return pl.CostEstimate(flops=int(micros * 1.1e9), bytes_accessed=int(micros * 3e6), transcendentals=0)


def put_halves(value, keep, send):
    rows = value.shape[0] // 2
    first = lax.rem(lax.axis_index("seq"), 2) == 0
    top, bottom = value[:rows], value[rows:]
    keep[...] = jnp.where(first, top, bottom)
    send[...] = jnp.where(first, bottom, top)


class Copies:
    def __init__(self, sems):
        self.sems, self.all = sems, []

    def start(self, source, target):
        copy = pltpu.make_async_copy(source, target, self.sems.at[len(self.all)])
        copy.start()
        self.all.append(copy)
        return copy

    def lanes(self, lanes, *pairs):
        return [
            [self.start(lane_of(source, lane, lanes), lane_of(target, lane, lanes)) for source, target in pairs]
            for lane in range(lanes)
        ]


def lane_of(ref, lane, lanes):
    if len(ref.shape) == 3:
        return ref.at[lane]
    rows = ref.shape[0] // lanes
    return ref.at[pl.ds(lane * rows, rows)]


def wait(copies):
    for copy in copies:
        copy.wait()


def first_kernel(
    short, bucket_hbm, assign_hbm, x_hbm, gain_hbm, b_hbm, gamma_hbm, nu_hbm, th_hbm,
    xs_hbm, normed_hbm, loc_hbm, pair_ref, pow_ref, keep_ref,
    bucket, assign, x_ref, gain_ref, b_ref, gamma_ref, nu_ref, th_ref, xs_ref, normed_ref, loc_ref, sems,
):
    lanes, seg, width = x_ref.shape
    span = seg // CHUNKS
    copies = Copies(sems)
    x_here = copies.lanes(lanes, (x_hbm, x_ref))
    nu_here, th_here = copies.start(nu_hbm, nu_ref), copies.start(th_hbm, th_ref)
    gain_here, gamma_here = copies.start(gain_hbm, gain_ref), copies.start(gamma_hbm, gamma_ref)
    b_here = copies.start(b_hbm, b_ref)
    tables = copies.start(bucket_hbm, bucket), copies.start(assign_hbm, assign)
    leaving = []

    order = scan_order(seg)
    nu_here.wait(), th_here.wait()
    modulus = jnp.exp(-jnp.exp(nu_ref[...]))
    phase = jnp.exp(th_ref[...])
    cstore(pow_ref, 0, (modulus * jnp.cos(phase), modulus * jnp.sin(phase)))
    size = 1
    while size < span:
        cstore(pow_ref, size, cmul(cload(pow_ref, 0, size), cload(pow_ref, size - 1)))
        size *= 2

    gain_here.wait(), gamma_here.wait()
    lam = cload(pow_ref, 0)
    lam_span = cload(pow_ref, span - 1)
    ends = []
    factor = jnp.exp(gamma_ref[...])
    factor = jnp.concatenate([factor, factor], 1)
    for lane in range(lanes):
        rows = pl.ds(lane * seg, seg)
        wait(x_here[lane])
        x = dot_nn(order, x_ref[lane])
        xs_ref[rows, :] = x.astype(BF16)
        xhat, _ = norm_stats(x)
        low = (xhat * gain_ref[...]).astype(BF16)
        normed_ref[rows, :] = low
        if lane == 0:
            b_here.wait()
        loc_ref[rows, :] = dot_nn(low, b_ref[...]) * factor
        for source, target in ((xs_ref, xs_hbm), (normed_ref, normed_hbm)):
            leaving.append(copies.start(source.at[rows], target.at[rows]))
        h = cload(loc_ref, lane * seg, CHUNKS)
        for step in range(1, span):
            at = lane * seg + step * CHUNKS
            h = fma(lam, h, cload(loc_ref, at, CHUNKS))
            cstore(loc_ref, at, h)
        leaving.append(copies.start(loc_ref.at[rows], loc_hbm.at[rows]))
        ends.append(h)

    wait(tables)
    fill_keeps(bucket, assign, keep_ref, lanes, seg, short)
    for lane, h in enumerate(ends):
        state = h[0][0:1], h[1][0:1]
        decay = kept(keep_ref, lane * CHUNKS, lam_span)
        for chunk in range(1, CHUNKS):
            step = kept(keep_ref, lane * CHUNKS + chunk, lam_span)
            state = fma(step, state, (h[0][chunk : chunk + 1], h[1][chunk : chunk + 1]))
            decay = cmul(step, decay)
        cstore(pair_ref, lane, state)
        cstore(pair_ref, lanes + lane, decay)
    wait(leaving)


def order_kernel(ct_hbm, cts_hbm, ct_ref, cts_ref, sems):
    lanes, seg, _ = ct_ref.shape
    copies = Copies(sems)
    here = copies.lanes(lanes, (ct_hbm, ct_ref))
    order = scan_order(seg)
    leaving = []
    for lane in range(lanes):
        rows = pl.ds(lane * seg, seg)
        wait(here[lane])
        cts_ref[rows, :] = dot_nn(order, ct_ref[lane]).astype(BF16)
        leaving.append(copies.start(cts_ref.at[rows], cts_hbm.at[rows]))
    wait(leaving)


def block_kernel(
    w_hbm, c_hbm, d_hbm, xs_hbm, normed_hbm, loc_hbm, cts_hbm, enter_ref, pow_ref, keep_ref,
    out_hbm, h_hbm, mixed_hbm, adj_hbm, carry_hbm, c_go_hbm, back_ref, g_d_ref, w_go_ref, w_send_ref, c_send_ref,
    carry_ref, c_go_ref, w_ref, c_ref, d_ref, xs_ref, normed_ref, h_ref, cts_ref,
    out_ref, states_ref, gelu_ref, pre_ref, slope_ref, mixed_ref, low_ref, adj_ref, sems,
):
    lanes, width = enter_ref.shape[0], d_ref.shape[1]
    seg = h_ref.shape[0] // lanes
    span = seg // CHUNKS
    copies = Copies(sems)
    one, rest = pl.ds(0, seg), pl.ds(seg, (lanes - 1) * seg)
    arrays = (loc_hbm, h_ref), (normed_hbm, normed_ref), (xs_hbm, xs_ref), (cts_hbm, cts_ref)
    loc_here = copies.start(loc_hbm.at[one], h_ref.at[one])
    c_here, d_here = copies.start(c_hbm, c_ref), copies.start(d_hbm, d_ref)
    normed_here = copies.start(normed_hbm.at[one], normed_ref.at[one])
    w_here = copies.start(w_hbm, w_ref)
    late_here = [copies.start(a.at[one], b.at[one]) for a, b in arrays[2:]]
    rest_here = [copies.start(a.at[rest], b.at[rest]) for a, b in arrays]
    leaving = []
    lam_span = cload(pow_ref, span - 1)
    for lane in range(lanes):
        first = lane * seg
        rows = pl.ds(first, seg)
        if lane == 0:
            loc_here.wait()
        elif lane == 1:
            wait(rest_here)
        last = first + (span - 1) * CHUNKS
        state = kept(keep_ref, lane * CHUNKS, cload(enter_ref, lane))
        cstore(carry_ref, lane * CHUNKS, state)
        for chunk in range(1, CHUNKS):
            state = fma(lam_span, state, cload(h_ref, last + chunk - 1))
            state = kept(keep_ref, lane * CHUNKS + chunk, state)
            cstore(carry_ref, lane * CHUNKS + chunk, state)
        carry = cload(carry_ref, lane * CHUNKS, CHUNKS)
        for step in range(span):
            at = first + step * CHUNKS
            cstore(h_ref, at, fma(cload(pow_ref, step), carry, cload(h_ref, at, CHUNKS)))
        leaving.append(copies.start(h_ref.at[rows], h_hbm.at[rows]))

        states = h_ref[rows, :].astype(BF16)
        states_ref[rows, :] = states
        if lane == 0:
            wait([normed_here, c_here, d_here])
        mixed = dot_nn(states, c_ref[...]) + d_ref[...] * normed_ref[rows, :].astype(F32)
        square = mixed * mixed
        tanh = jnp.tanh(GELU_K * mixed * (1.0 + GELU_A * square))
        half_up = 0.5 * (1.0 + tanh)
        gelu = (mixed * half_up).astype(BF16)
        gelu_ref[rows, :] = gelu
        slope_ref[rows, :] = half_up + 0.5 * GELU_K * mixed * (1.0 - tanh * tanh) * (
            1.0 + 3.0 * GELU_A * square
        )
        if lane == 0:
            w_here.wait()
        pre = dot_nn(gelu, w_ref[...])
        value = pre[:, :width]
        sig = jax.nn.sigmoid(pre[:, width:])
        gated = value * sig
        if lane == 0:
            wait(late_here)
        out_ref[rows, :] = (xs_ref[rows, :].astype(F32) + gated).astype(BF16)
        leaving.append(copies.start(out_ref.at[rows], out_hbm.at[rows]))
        grad_value = cts_ref[rows, :].astype(F32) * sig
        pre_ref[rows, :width] = grad_value.astype(BF16)
        pre_ref[rows, width:] = (grad_value * (value - gated)).astype(BF16)

    lam, lam_span = conj(cload(pow_ref, 0)), conj(lam_span)
    total = None
    for lane in range(lanes):
        rows = pl.ds(lane * seg, seg)
        grad_mixed = dot_nt(pre_ref[rows, :], w_ref[...]) * slope_ref[rows, :]
        mixed_ref[rows, :] = grad_mixed
        leaving.append(copies.start(mixed_ref.at[rows], mixed_hbm.at[rows]))
        add = jnp.sum(grad_mixed * normed_ref[rows, :].astype(F32), axis=0, keepdims=True)
        total = add if total is None else total + add
        low = grad_mixed.astype(BF16)
        low_ref[rows, :] = low
        adj_ref[rows, :] = dot_nt(low, c_ref[...])
        adj = cload(adj_ref, (lane + 1) * seg - CHUNKS, CHUNKS)
        for step in reversed(range(span - 1)):
            at = lane * seg + step * CHUNKS
            adj = fma(lam, adj, cload(adj_ref, at, CHUNKS))
            cstore(adj_ref, at, adj)
        leaving.append(copies.start(adj_ref.at[rows], adj_hbm.at[rows]))
        state = None
        for chunk in reversed(range(CHUNKS)):
            here = adj[0][chunk : chunk + 1], adj[1][chunk : chunk + 1]
            state = here if state is None else fma(lam_span, state, here)
            state = kept(keep_ref, lane * CHUNKS + chunk, state)
        cstore(back_ref, lane, state)
    g_d_ref[...] = total
    leaving.append(copies.start(carry_ref, carry_hbm))
    put_halves(dot_tn(states_ref[...], low_ref[...]), c_go_ref, c_send_ref)
    leaving.append(copies.start(c_go_ref, c_go_hbm))
    put_halves(dot_tn(gelu_ref[...], pre_ref[...]), w_go_ref, w_send_ref)
    wait(leaving)


def states_kernel(
    c_go_hbm, h_hbm, adj_hbm, normed_hbm, carry_ref, b_ref, gamma_ref, d_ref, leave_ref, pow_ref, keep_ref, g_d_ref,
    c_got_ref,
    low_hbm, go_ref, send_ref, c_ref, h_ref, adj_ref, normed_ref, low_ref, after_ref, small_ref, sems,
):
    copies = Copies(sems)
    h_here = copies.lanes(leave_ref.shape[0], (adj_hbm, adj_ref), (h_hbm, h_ref))
    normed_here = copies.start(normed_hbm, normed_ref)
    c_here = copies.start(c_go_hbm, c_ref)
    leaving = []
    lanes = leave_ref.shape[0]
    seg = normed_ref.shape[0] // lanes
    span = seg // CHUNKS
    back = conj(cload(pow_ref, span - 1))
    factor = jnp.exp(gamma_ref[...])
    sums = None
    for lane in range(lanes):
        first = lane * seg
        state = cload(leave_ref, lane)
        wait(h_here[lane])
        cstore(after_ref, CHUNKS - 1, state)
        for chunk in reversed(range(1, CHUNKS)):
            state = fma(back, state, cload(adj_ref, first + chunk))
            state = kept(keep_ref, lane * CHUNKS + chunk, state)
            cstore(after_ref, chunk - 1, state)
        after = cload(after_ref, 0, CHUNKS)
        before = cload(carry_ref, lane * CHUNKS, CHUNKS)
        for step in range(span):
            at = first + step * CHUNKS
            full = fma(conj(cload(pow_ref, span - 1 - step)), after, cload(adj_ref, at, CHUNKS))
            add = cmul(conj(before), full)
            sums = add if sums is None else cadd(sums, add)
            cstore(low_ref, at, ((full[0] * factor).astype(BF16), (full[1] * factor).astype(BF16)))
            before = cload(h_ref, at, CHUNKS)
        rows = pl.ds(first, seg)
        leaving.append(copies.start(low_ref.at[rows], low_hbm.at[rows]))
    normed_here.wait()
    grad_b = dot_tn(normed_ref[...], low_ref[...])
    n = gamma_ref.shape[1]
    prod = grad_b * b_ref[...].astype(F32)
    small_ref[...] = jnp.zeros_like(small_ref)
    small_ref[0:1, :n] = jnp.sum(sums[0], axis=0, keepdims=True)
    small_ref[0:1, n:] = jnp.sum(sums[1], axis=0, keepdims=True)
    small_ref[1:2, :] = jnp.sum(prod, axis=0, keepdims=True)
    small_ref[8:9, :] = jnp.sum(prod.T, axis=0, keepdims=True) + d_ref[...] * g_d_ref[...]
    small_ref[9:10, :] = g_d_ref[...]
    put_halves(grad_b, go_ref.at[pl.ds(0, n)], send_ref.at[pl.ds(0, n)])
    put_halves(small_ref[...], go_ref.at[pl.ds(n, 8)], send_ref.at[pl.ds(n, 8)])
    c_here.wait()
    c_ref[...] += c_got_ref[...]
    wait(leaving)


def put_pieces(get, own_ref, send_refs):
    rows = own_ref.shape[0]
    mine = lax.axis_index("dp")
    for mask, ref in enumerate((own_ref, *send_refs)):
        ref[:rows, :] = get(pl.ds(pl.multiple_of((mine ^ mask) * rows, rows), rows))


def c_pieces_kernel(c_ref, own_ref, *send_refs):
    put_pieces(lambda at: c_ref[at, :], own_ref, send_refs)


def b_pieces_kernel(keep_ref, got_ref, small_ref, own_ref, *send_refs):
    n = own_ref.shape[0] * (len(send_refs) + 1)
    small = keep_ref[n:, :] + got_ref[n:, :]
    small_ref[...] = small
    put_pieces(lambda at: keep_ref[at, :] + got_ref[at, :], own_ref, send_refs)
    for ref in send_refs:
        ref[own_ref.shape[0] :, :] = small


def split_kernel(phase, keep_ref, got_ref, own_ref, send_ref):
    rows = own_ref.shape[0]
    mine = my_bit(phase)
    if rows % 8:
        total = keep_ref[...] + got_ref[...]
        own_ref[...] = jnp.where(mine == 0, total[:rows], total[rows:])
        send_ref[...] = jnp.where(mine == 0, total[rows:], total[:rows])
        return
    for ref, which in ((own_ref, mine), (send_ref, 1 - mine)):
        at = pl.ds(pl.multiple_of(which * rows, rows), rows)
        ref[...] = keep_ref[at, :] + got_ref[at, :]


def input_kernel(
    gain_hbm, b_hbm, d_hbm, xs_hbm, cts_hbm, low_hbm, mixed_hbm, out_hbm,
    in_hbm, block_hbm, gain_ref, b_ref, d_ref, xs_ref, cts_ref, low_ref, mixed_ref, out_ref,
    in_ref, block_ref, sems,
):
    lanes, seg, width = in_ref.shape
    copies = Copies(sems)
    params = [copies.start(a, b) for a, b in ((gain_hbm, gain_ref), (b_hbm, b_ref), (d_hbm, d_ref))]
    here = copies.lanes(
        lanes, (low_hbm, low_ref), (mixed_hbm, mixed_ref), (xs_hbm, xs_ref), (cts_hbm, cts_ref),
        (out_hbm, out_ref),
    )
    wait(params)
    leaving = []
    order_back = scan_order(seg, True)
    for lane in range(lanes):
        rows = pl.ds(lane * seg, seg)
        wait(here[lane])
        grad_normed = dot_nt(low_ref[rows, :], b_ref[...]) + mixed_ref[rows, :] * d_ref[...]
        xhat, scale = norm_stats(xs_ref[rows, :].astype(F32))
        dxhat = grad_normed * gain_ref[...]
        one = jnp.mean(dxhat, axis=-1, keepdims=True)
        two = jnp.mean(dxhat * xhat, axis=-1, keepdims=True)
        grad = (cts_ref[rows, :].astype(F32) + (dxhat - one - xhat * two) * scale).astype(BF16)
        in_ref[lane] = dot_nn(order_back, grad).astype(BF16)
        leaving.append(copies.start(in_ref.at[lane], in_hbm.at[lane]))
        block_ref[lane] = dot_nn(order_back, out_ref[rows, :]).astype(BF16)
        leaving.append(copies.start(block_ref.at[lane], block_hbm.at[lane]))
    wait(leaving)


def finish_kernel(
    nu_hbm, th_hbm, gain_hbm, small_ref, pow_ref, gain_out, gamma_out, nu_out, th_out, d_out,
    nu_ref, th_ref, gain_ref, sems,
):
    n = nu_ref.shape[1]
    copies = Copies(sems)
    for copy in [copies.start(a, b) for a, b in ((nu_hbm, nu_ref), (th_hbm, th_ref), (gain_hbm, gain_ref))]:
        copy.wait()
    lam = cload(pow_ref, 0)
    p, q = small_ref[0:1, :n], small_ref[0:1, n:]
    nu_out[...] = -jnp.exp(nu_ref[...]) * (p * lam[0] + q * lam[1])
    th_out[...] = -jnp.exp(th_ref[...]) * (p * lam[1] - q * lam[0])
    gamma_out[...] = small_ref[1:2, :n] + small_ref[1:2, n:]
    gain_out[...] = small_ref[8:9, :] / gain_ref[...]
    d_out[...] = small_ref[9:10, :]


def swap(value, axis, bit):
    count = lax.axis_size(axis)
    return lax.ppermute(value, axis, [(i, i ^ (1 << bit)) for i in range(count)])


def entering(pair, backward, beside=None):
    lanes, n = pair.shape[0] // 2, pair.shape[1] // 2

    def mul(x, y):
        return jnp.concatenate(
            [x[:, :n] * y[:, :n] - x[:, n:] * y[:, n:], x[:, :n] * y[:, n:] + x[:, n:] * y[:, :n]], 1
        )

    def join(early, late):
        return late[0] + mul(late[1], early[0]), mul(late[1], early[1])

    count, mine = lax.axis_size("seq"), lax.axis_index("seq")
    one = jnp.concatenate([jnp.ones_like(pair[:lanes, :n]), jnp.zeros_like(pair[:lanes, n:])], 1)
    before = jnp.zeros_like(one), one
    bit = 0
    while 1 << bit < count:
        size = 2 if bit == 0 else min(4, count >> bit)
        if beside is not None and bit == (1 if not backward else 0):
            pair, beside = tie(pair, beside)
        parts = [pair] + [
            lax.ppermute(pair, "seq", [(i, i ^ (mask << bit)) for i in range(count)])
            for mask in reversed(range(1, size))
        ][::-1]
        place = mine // (1 << bit) % size ^ (size - 1 if backward else 0)
        ordered = []
        for k in range(size):
            part = parts[0]
            for mask in range(1, size):
                part = jnp.where(place ^ k == mask, parts[mask], part)
            ordered.append((part[:lanes], part[lanes:]))
        sofar = None
        for k, item in enumerate(ordered):
            if k:
                joined = join(sofar, before)
                before = tuple(jnp.where(place == k, new, old) for new, old in zip(joined, before))
            sofar = item if sofar is None else join(sofar, item)
        pair = jnp.concatenate(sofar, 0)
        bit += size.bit_length() - 1
    return before[0] if beside is None else (before[0], beside)


def bits(axis, first=0):
    return [(axis, bit) for bit in range(first, lax.axis_size(axis).bit_length() - 1)]


def phases(first=False):
    dp, far = bits("dp"), bits("seq", 1)
    if first:
        return [dp + far, dp[::-1] + far]
    return [dp + far, dp[::-1] + far]


def hop(value, phase):
    orders, count = phases(phase < 0), lax.axis_size("seq")
    phase = phase if phase >= 0 else -1 - phase
    pairs = []
    for device in range(lax.axis_size("dp") * count):
        axis, bit = orders[device % 2][phase]
        pairs.append((device, device ^ ((1 << bit) * (count if axis == "dp" else 1))))
    return lax.ppermute(value, ("dp", "seq"), pairs)


def my_bit(phase):
    place = phase if phase >= 0 else -1 - phase
    one, two = (lax.axis_index(axis) // (1 << bit) % 2 for axis, bit in (o[place] for o in phases(phase < 0)))
    return jnp.where(lax.axis_index("seq") % 2 == 0, one, two)


def piece(value, which, count):
    rows = value.shape[1] // count
    return lax.dynamic_slice(value, (0, which * rows, 0), (value.shape[0], rows, value.shape[2]))


def pack(value, extra):
    if extra is None:
        return value
    return jnp.concatenate([value.reshape(-1, value.shape[2]), extra], 0)


def unpack(sent, value, extra):
    if extra is None:
        return sent, None
    rows = value.shape[0] * value.shape[1]
    return sent[:rows].reshape(value.shape), sent[rows:]


def tree_sum(values):
    while len(values) > 1:
        values = [a + b for a, b in zip(values[::2], values[1::2])]
    return values[0]


def scatter(value, phase, extra=None):
    mine = my_bit(phase)
    send, keep = piece(value, 1 - mine, 2), piece(value, mine, 2)
    got, more = unpack(hop(pack(send, extra), phase), send, extra)
    return keep + got, None if extra is None else extra + more


def double(value, phase, extra=None):
    got, more = unpack(hop(pack(value, extra), phase), value, extra)
    return value + got, None if extra is None else extra + more


def gather(value, phase):
    got = hop(value, phase)
    return join_rows([value, got], my_bit(phase))


def join_rows(parts, mine):
    count = len(parts)
    if count == 1:
        return parts[0]
    half = count // 2
    low = join_rows(parts[:half], mine % half)
    high = join_rows(parts[half:], mine % half)
    first = mine // half == 0
    return jnp.where(first, jnp.concatenate([low, high], 1), jnp.concatenate([high, low], 1))


def across(value, mask):
    return lax.ppermute(value, "dp", [(i, i ^ mask) for i in range(lax.axis_size("dp"))])


def sum_dp(own, sends, extra):
    parts, extras = [own], [extra]
    for mask, send in enumerate(sends):
        got, more = unpack(across(send, mask + 1), own, extra)
        parts.append(got)
        extras.append(more)
    return tree_sum(parts), None if extra is None else tree_sum(extras)


def gather_dp(value):
    count, mine = lax.axis_size("dp"), lax.axis_index("dp")
    parts = [value]
    for mask in reversed(range(1, count)):
        parts.insert(1, across(value, mask))
    return join_rows(parts, mine)


def only(step):
    return lambda value, extra=None: (step(value), extra)


def tie(*values):
    return lax.optimization_barrier(values)


def after(value, *others):
    for other in others:
        value = value + jnp.minimum(jnp.abs(other[(0,) * other.ndim]), 0.0)
    return value


def assemble_kernel(mine, other, *refs):
    whole, sems = refs[:-1], refs[-1]
    copies = Copies(sems)
    rows = mine.shape[0]
    first = pl.multiple_of(lax.rem(lax.axis_index("seq"), 2) * rows, rows)
    column = 0
    for out in whole:
        columns = pl.ds(column, out.shape[1])
        copies.start(mine.at[:, columns], out.at[pl.ds(first, rows)])
        copies.start(other.at[:, columns], out.at[pl.ds(pl.multiple_of(rows - first, rows), rows)])
        column += out.shape[1]
    wait(copies.all)


def on_device(
    block_in, cotangent, bucket_id, assignment, norm_gain, b_proj, gamma_log, nu_log, theta_log,
    c_proj, d_skip, glu_weight,
):
    _, lanes, seg, width = block_in.shape
    n = nu_log.shape[0]
    two = 2 * n
    tokens = lanes * seg
    span = seg // CHUNKS
    short = seg * lax.axis_size("seq") // bucket_id.shape[2]
    gain, gamma, nu, theta, skip = (
        v.reshape(1, -1) for v in (norm_gain, gamma_log, nu_log, theta_log, d_skip)
    )
    hbm, vmem = pl.BlockSpec(memory_space=pltpu.HBM), pl.BlockSpec(memory_space=pltpu.VMEM)

    def call(kernel, name, micros, outs, far, near, fetched=None, scratch=(), sems=0, far_outs=0, limit=4, pin=False, wait_for=()):
        fetched = far if fetched is None else fetched
        far = [pltpu.with_memory_space_constraint(v, pltpu.HBM) for v in far]
        if pin:
            near = [pltpu.with_memory_space_constraint(v, pltpu.VMEM) for v in near]
        shapes = [
            pltpu.HBM(shape, kind) if k < far_outs else jax.ShapeDtypeStruct(shape, kind)
            for k, (shape, kind) in enumerate(outs)
        ]
        room = [(pltpu.SMEM if v.dtype == jnp.int32 else pltpu.VMEM)(v.shape, v.dtype) for v in fetched]
        count, extra = len(far) + len(near), len(wait_for)

        def body(*refs):
            kernel(*refs[:count], *refs[count + extra :])

        return pl.pallas_call(
            body,
            in_specs=[hbm] * len(far) + [vmem] * len(near) + [pl.BlockSpec(memory_space=pl.ANY)] * extra,
            out_specs=[hbm] * far_outs + [vmem] * (len(outs) - far_outs),
            out_shape=shapes,
            scratch_shapes=room
            + [pltpu.VMEM(shape, kind) for shape, kind in scratch]
            + ([pltpu.SemaphoreType.DMA((sems,))] if sems else []),
            compiler_params=pltpu.CompilerParams(vmem_limit_bytes=limit * 1024 * 1024),
            cost_estimate=cost(micros),
            name=name,
        )(*far, *near, *wait_for)

    low_rows, full_rows = ((tokens, width), BF16), ((tokens, two), F32)
    lane_rows = ((lanes, seg, width), BF16)
    xs, normed, loc, pair, powers, keep = call(
        functools.partial(first_kernel, short), "forward_local", 4,
        [
            low_rows, low_rows, full_rows, ((2 * lanes, two), F32), ((span, two), F32),
            ((lanes * CHUNKS, two), F32),
        ],
        [bucket_id[0], assignment, block_in[0], gain, b_proj, gamma, nu, theta], [],
        scratch=[low_rows, low_rows, full_rows], sems=4 * lanes + 7, far_outs=3, limit=12,
    )
    enter, cotangent_later = entering(pair, False, cotangent[0])
    (cts,) = call(
        order_kernel, "cotangent_order", 2, [low_rows], [cotangent_later], [],
        scratch=[low_rows], sems=2 * lanes, far_outs=1, limit=8,
    )

    chunk_rows, half_rows = ((lanes * CHUNKS, two), F32), ((n, width), F32)
    out, h, grad_mixed, adj, carry, c_keep, back_total, grad_d, w_keep, w_send, c_send = call(
        block_kernel, "block", 10,
        [
            low_rows, full_rows, full_rows, full_rows, chunk_rows, half_rows, ((lanes, two), F32),
            ((1, width), F32), ((n, 2 * width), F32), ((n, 2 * width), F32), half_rows,
        ],
        [glu_weight, c_proj, skip, xs, normed, loc, cts], [enter, powers, keep], fetched=(),
        scratch=[
            chunk_rows, half_rows, ((width, 2 * width), BF16), ((two, width), BF16), ((1, width), F32),
            low_rows, low_rows, full_rows, low_rows,
            low_rows, low_rows, low_rows, ((tokens, 2 * width), BF16), full_rows, full_rows, low_rows,
            full_rows,
        ],
        sems=4 * lanes + 13, far_outs=6, limit=36,
    )

    decay = pair[lanes:]
    back_pair = jnp.concatenate(
        [back_total, jnp.concatenate([decay[:, :n], -decay[:, n:]], 1)], 0
    )
    near, last = len(bits("dp")), len(phases()[0]) - 1
    c_got = swap(c_send, "seq", 0)

    def split(keep, got, phase):
        half = ((keep.shape[0] // 2, keep.shape[1]), F32)
        return call(
            functools.partial(split_kernel, phase), "split_sum", 0.5, [half, half], [], [keep, got], pin=True
        )

    own, send = split(w_keep, swap(w_send, "seq", 0), -1)
    leave, own = entering(back_pair, True, own)
    owns = [own]
    for phase in range(1, last):
        own, send = split(own, hop(send, -phase), -1 - phase)
        owns.append(own)
    w = (own + hop(send, -last))[None]
    w_steps = [functools.partial(double, phase=-1 - last)]
    w_steps += [only(functools.partial(gather, phase=-1 - p)) for p in reversed(range(last))]
    for step in w_steps:
        w, _ = step(w)

    back_low, b_keep, b_send, c = call(
        states_kernel, "adjoint_states", 3,
        [low_rows, ((n + 8, two), F32), ((n + 8, two), F32), half_rows],
        [c_keep, h, adj, normed], [carry, b_proj, gamma, skip, leave, powers, keep, grad_d, c_got], fetched=(),
        scratch=[full_rows, full_rows, low_rows, low_rows, ((CHUNKS, two), F32), ((16, two), F32)],
        sems=3 * lanes + 2, far_outs=1, limit=14, wait_for=[owns[1]],
    )

    def back_input(back_low):
        return call(
            input_kernel, "back_input", 4, [lane_rows, lane_rows],
            [gain, b_proj, skip, xs, cts, back_low, grad_mixed, out], [], wait_for=[cb, finished[0], w],
            scratch=[lane_rows, lane_rows], sems=7 * lanes + 3, far_outs=2, limit=12,
        )

    groups = lax.axis_size("dp")
    cut = n // groups
    piece_rows = ((cut, width), F32)
    c_own, *c_sends = call(c_pieces_kernel, "c_pieces", 0.5, [piece_rows] * groups, [], [c])
    c, _ = sum_dp(c_own[None], [v[None] for v in c_sends], None)
    small, b_own, *b_sends = call(
        b_pieces_kernel, "b_pieces", 0.5,
        [((8, two), F32), piece_rows] + [((cut + 8, width), F32)] * (groups - 1),
        [], [b_keep, swap(b_send, "seq", 0)], wait_for=[owns[2]],
    )
    b, small = sum_dp(b_own[None], b_sends, small)
    cb = jnp.concatenate([c, b], 0)

    steps = [functools.partial(scatter, phase=p) for p in range(near, last)]
    steps += [functools.partial(double, phase=last)]
    steps += [only(functools.partial(gather, phase=p)) for p in reversed(range(near, last))]
    for step in steps:
        cb, small = step(cb, extra=small)
    got = swap(small, "seq", 0)
    small = join_rows([small[None], got[None]], lax.axis_index("seq") % 2)[0]
    finished = call(
        finish_kernel, "finish", 1, [((1, v), F32) for v in (width, n, n, n, width)],
        [nu, theta, gain], [small, powers], sems=3,
    )
    grad_in, block_out = back_input(back_low)
    cb, w = tie(cb, w)
    cb = gather_dp(cb)
    cb, grad_in, block_out = tie(cb, grad_in, block_out)
    w, cb = w[0], jnp.concatenate([cb[0], cb[1]], 1)

    grad_gain, grad_gamma, grad_nu, grad_theta, grad_d = finished

    def assemble(mine, widths, wait_for):
        return call(
            assemble_kernel, "assemble", 2, [((2 * mine.shape[0], v), F32) for v in widths],
            [], [mine, swap(mine, "seq", 0)], sems=2 * len(widths), far_outs=len(widths), pin=True, wait_for=wait_for,
        )

    (grad_w,) = assemble(w, [2 * width], [grad_in])
    grad_c, grad_b = assemble(cb, [width, two], [])
    return (
        block_out[None], grad_in[None], grad_gain[0], grad_b, grad_gamma[0], grad_nu[0], grad_theta[0],
        grad_c, grad_d[0], grad_w,
    )


def solution(mesh):
    rows = P("dp", None, "seq", None)
    in_specs = (rows, rows, P("dp", None, None), P("dp", None)) + (P(),) * 8
    out_specs = (rows, rows) + (P(),) * 8
    return jax.shard_map(
        on_device, mesh=mesh, in_specs=in_specs, out_specs=out_specs, check_vma=False
    )
```

```python
import functools

import jax
import jax.numpy as jnp
from jax import lax
from jax.experimental import pallas as pl
from jax.experimental.pallas import tpu as pltpu
from jax.sharding import PartitionSpec as P

EPS = 1e-05
CHUNKS = 8
GELU_A = 0.044715
GELU_K = 0.7978845608028654
F32 = jnp.float32
BF16 = jnp.bfloat16


def dot_nt(left, right):
    return lax.dot_general(left, right, (((1,), (1,)), ((), ())), preferred_element_type=F32)


def dot_tn(left, right):
    return lax.dot_general(left, right, (((0,), (0,)), ((), ())), preferred_element_type=F32)


def dot_nn(left, right):
    return jnp.dot(left, right, preferred_element_type=F32)


def cmul(x, y):
    return x[0] * y[0] - x[1] * y[1], x[0] * y[1] + x[1] * y[0]


def cadd(x, y):
    return x[0] + y[0], x[1] + y[1]


def fma(a, x, y):
    return (y[0] - a[1] * x[1]) + a[0] * x[0], (y[1] + a[1] * x[0]) + a[0] * x[1]


def conj(x):
    return x[0], -x[1]


def cload(ref, first, count=1):
    n = ref.shape[-1] // 2
    return ref[first : first + count, :n], ref[first : first + count, n:]


def cstore(ref, first, value):
    n = ref.shape[-1] // 2
    rows = value[0].shape[0]
    ref[first : first + rows, :n], ref[first : first + rows, n:] = value


def kept(ref, row, value):
    keep = cload(ref, row)
    return value[0] * keep[0], value[1] * keep[1]


def scan_order(seg, back=False):
    row = lax.broadcasted_iota(jnp.int32, (seg, seg), 0)
    column = lax.broadcasted_iota(jnp.int32, (seg, seg), 1)
    if back:
        row, column = column, row
    span = seg // CHUNKS
    hit = (row % CHUNKS == column // span) & (row // CHUNKS == column % span)
    return jnp.where(hit, 1.0, 0.0).astype(BF16)


def fill_keeps(bucket, assign, keep_ref, lanes, seg, short):
    own = lax.axis_index("seq")
    for lane in range(lanes):
        pattern = assign[0, lane]
        for chunk in range(CHUNKS):
            token = own * seg + chunk * (seg // CHUNKS)
            here = bucket[pattern, lax.div(token, short)]
            span = jnp.where(here == 0, short, jnp.where(here == 1, 4 * short, 16 * short))
            keep = jnp.where(lax.rem(token, span) == 0, 0.0, 1.0).astype(F32)
            row = lane * CHUNKS + chunk
            keep_ref[row : row + 1, :] = jnp.full((1, keep_ref.shape[1]), keep)


def norm_stats(rows):
    mean = jnp.mean(rows, axis=-1, keepdims=True)
    centred = rows - mean
    var = jnp.mean(centred * centred, axis=-1, keepdims=True)
    scale = lax.rsqrt(var + EPS)
    return centred * scale, scale


def cost(micros):
    return pl.CostEstimate(flops=int(micros * 1.1e9), bytes_accessed=int(micros * 3e6), transcendentals=0)


def put_halves(value, keep, send):
    rows = value.shape[0] // 2
    first = lax.rem(lax.axis_index("seq"), 2) == 0
    top, bottom = value[:rows], value[rows:]
    keep[...] = jnp.where(first, top, bottom)
    send[...] = jnp.where(first, bottom, top)


def half_tn(left, right, other):
    columns = left.shape[1] // 2
    first = lax.rem(lax.axis_index("seq"), 2) == other
    return dot_tn(jnp.where(first, left[:, :columns], left[:, columns:]), right)


class Copies:
    def __init__(self, sems):
        self.sems, self.all = sems, []

    def start(self, source, target):
        copy = pltpu.make_async_copy(source, target, self.sems.at[len(self.all)])
        copy.start()
        self.all.append(copy)
        return copy

    def lanes(self, lanes, *pairs):
        return [
            [self.start(lane_of(source, lane, lanes), lane_of(target, lane, lanes)) for source, target in pairs]
            for lane in range(lanes)
        ]


def lane_of(ref, lane, lanes):
    if len(ref.shape) == 3:
        return ref.at[lane]
    rows = ref.shape[0] // lanes
    return ref.at[pl.ds(lane * rows, rows)]


def wait(copies):
    for copy in copies:
        copy.wait()


def first_kernel(
    short, bucket_hbm, assign_hbm, x_hbm, gain_hbm, b_hbm, gamma_hbm, nu_hbm, th_hbm,
    xs_hbm, normed_hbm, loc_hbm, pair_ref, pow_ref, keep_ref,
    bucket, assign, x_ref, gain_ref, b_ref, gamma_ref, nu_ref, th_ref, xs_ref, normed_ref, loc_ref, sems,
):
    lanes, seg, width = x_ref.shape
    span = seg // CHUNKS
    copies = Copies(sems)
    x_here = copies.lanes(lanes, (x_hbm, x_ref))
    nu_here, th_here = copies.start(nu_hbm, nu_ref), copies.start(th_hbm, th_ref)
    gain_here, gamma_here = copies.start(gain_hbm, gain_ref), copies.start(gamma_hbm, gamma_ref)
    b_here = copies.start(b_hbm, b_ref)
    tables = copies.start(bucket_hbm, bucket), copies.start(assign_hbm, assign)
    leaving = []

    order = scan_order(seg)
    nu_here.wait(), th_here.wait()
    modulus = jnp.exp(-jnp.exp(nu_ref[...]))
    phase = jnp.exp(th_ref[...])
    cstore(pow_ref, 0, (modulus * jnp.cos(phase), modulus * jnp.sin(phase)))
    size = 1
    while size < span:
        cstore(pow_ref, size, cmul(cload(pow_ref, 0, size), cload(pow_ref, size - 1)))
        size *= 2

    gain_here.wait(), gamma_here.wait()
    lam = cload(pow_ref, 0)
    lam_span = cload(pow_ref, span - 1)
    ends = []
    factor = jnp.exp(gamma_ref[...])
    factor = jnp.concatenate([factor, factor], 1)
    for lane in range(lanes):
        rows = pl.ds(lane * seg, seg)
        wait(x_here[lane])
        x = dot_nn(order, x_ref[lane])
        xs_ref[rows, :] = x.astype(BF16)
        xhat, _ = norm_stats(x)
        low = (xhat * gain_ref[...]).astype(BF16)
        normed_ref[rows, :] = low
        if lane == 0:
            b_here.wait()
        loc_ref[rows, :] = dot_nn(low, b_ref[...]) * factor
        for source, target in ((xs_ref, xs_hbm), (normed_ref, normed_hbm)):
            leaving.append(copies.start(source.at[rows], target.at[rows]))
        h = cload(loc_ref, lane * seg, CHUNKS)
        for step in range(1, span):
            at = lane * seg + step * CHUNKS
            h = fma(lam, h, cload(loc_ref, at, CHUNKS))
            cstore(loc_ref, at, h)
        leaving.append(copies.start(loc_ref.at[rows], loc_hbm.at[rows]))
        ends.append(h)

    wait(tables)
    fill_keeps(bucket, assign, keep_ref, lanes, seg, short)
    for lane, h in enumerate(ends):
        state = h[0][0:1], h[1][0:1]
        decay = kept(keep_ref, lane * CHUNKS, lam_span)
        for chunk in range(1, CHUNKS):
            step = kept(keep_ref, lane * CHUNKS + chunk, lam_span)
            state = fma(step, state, (h[0][chunk : chunk + 1], h[1][chunk : chunk + 1]))
            decay = cmul(step, decay)
        cstore(pair_ref, lane, state)
        cstore(pair_ref, lanes + lane, decay)
    wait(leaving)


def order_kernel(ct_hbm, cts_hbm, ct_ref, cts_ref, sems):
    lanes, seg, _ = ct_ref.shape
    copies = Copies(sems)
    here = copies.lanes(lanes, (ct_hbm, ct_ref))
    order = scan_order(seg)
    leaving = []
    for lane in range(lanes):
        rows = pl.ds(lane * seg, seg)
        wait(here[lane])
        cts_ref[rows, :] = dot_nn(order, ct_ref[lane]).astype(BF16)
        leaving.append(copies.start(cts_ref.at[rows], cts_hbm.at[rows]))
    wait(leaving)


def block_kernel(
    w_hbm, c_hbm, d_hbm, xs_hbm, normed_hbm, loc_hbm, cts_hbm, enter_ref, pow_ref, keep_ref,
    out_hbm, h_hbm, mixed_hbm, adj_hbm, carry_hbm, back_ref, g_d_ref, w_send_ref,
    states_ref, gelu_ref, pre_ref, low_ref, carry_ref, w_ref, c_ref, d_ref, xs_ref, normed_ref, h_ref, cts_ref,
    out_ref, slope_ref, mixed_ref, adj_ref, sems,
):
    lanes, width = enter_ref.shape[0], d_ref.shape[1]
    seg = h_ref.shape[0] // lanes
    span = seg // CHUNKS
    copies = Copies(sems)
    one, rest = pl.ds(0, seg), pl.ds(seg, (lanes - 1) * seg)
    arrays = (loc_hbm, h_ref), (normed_hbm, normed_ref), (xs_hbm, xs_ref), (cts_hbm, cts_ref)
    loc_here = copies.start(loc_hbm.at[one], h_ref.at[one])
    c_here, d_here = copies.start(c_hbm, c_ref), copies.start(d_hbm, d_ref)
    normed_here = copies.start(normed_hbm.at[one], normed_ref.at[one])
    w_here = copies.start(w_hbm, w_ref)
    late_here = [copies.start(a.at[one], b.at[one]) for a, b in arrays[2:]]
    rest_here = [copies.start(a.at[rest], b.at[rest]) for a, b in arrays]
    leaving = []
    lam_span = cload(pow_ref, span - 1)
    for lane in range(lanes):
        first = lane * seg
        rows = pl.ds(first, seg)
        if lane == 0:
            loc_here.wait()
        elif lane == 1:
            wait(rest_here)
        last = first + (span - 1) * CHUNKS
        state = kept(keep_ref, lane * CHUNKS, cload(enter_ref, lane))
        cstore(carry_ref, lane * CHUNKS, state)
        for chunk in range(1, CHUNKS):
            state = fma(lam_span, state, cload(h_ref, last + chunk - 1))
            state = kept(keep_ref, lane * CHUNKS + chunk, state)
            cstore(carry_ref, lane * CHUNKS + chunk, state)
        carry = cload(carry_ref, lane * CHUNKS, CHUNKS)
        for step in range(span):
            at = first + step * CHUNKS
            cstore(h_ref, at, fma(cload(pow_ref, step), carry, cload(h_ref, at, CHUNKS)))
        leaving.append(copies.start(h_ref.at[rows], h_hbm.at[rows]))

        states = h_ref[rows, :].astype(BF16)
        states_ref[rows, :] = states
        if lane == 0:
            wait([normed_here, c_here, d_here])
        mixed = dot_nn(states, c_ref[...]) + d_ref[...] * normed_ref[rows, :].astype(F32)
        square = mixed * mixed
        tanh = jnp.tanh(GELU_K * mixed * (1.0 + GELU_A * square))
        half_up = 0.5 * (1.0 + tanh)
        gelu = (mixed * half_up).astype(BF16)
        gelu_ref[rows, :] = gelu
        slope_ref[rows, :] = half_up + 0.5 * GELU_K * mixed * (1.0 - tanh * tanh) * (
            1.0 + 3.0 * GELU_A * square
        )
        if lane == 0:
            w_here.wait()
        pre = dot_nn(gelu, w_ref[...])
        value = pre[:, :width]
        sig = jax.nn.sigmoid(pre[:, width:])
        gated = value * sig
        if lane == 0:
            wait(late_here)
        out_ref[rows, :] = (xs_ref[rows, :].astype(F32) + gated).astype(BF16)
        leaving.append(copies.start(out_ref.at[rows], out_hbm.at[rows]))
        grad_value = cts_ref[rows, :].astype(F32) * sig
        pre_ref[rows, :width] = grad_value.astype(BF16)
        pre_ref[rows, width:] = (grad_value * (value - gated)).astype(BF16)

    lam, lam_span = conj(cload(pow_ref, 0)), conj(lam_span)
    total = None
    for lane in range(lanes):
        rows = pl.ds(lane * seg, seg)
        grad_mixed = dot_nt(pre_ref[rows, :], w_ref[...]) * slope_ref[rows, :]
        mixed_ref[rows, :] = grad_mixed
        leaving.append(copies.start(mixed_ref.at[rows], mixed_hbm.at[rows]))
        add = jnp.sum(grad_mixed * normed_ref[rows, :].astype(F32), axis=0, keepdims=True)
        total = add if total is None else total + add
        low = grad_mixed.astype(BF16)
        low_ref[rows, :] = low
        adj_ref[rows, :] = dot_nt(low, c_ref[...])
        adj = cload(adj_ref, (lane + 1) * seg - CHUNKS, CHUNKS)
        for step in reversed(range(span - 1)):
            at = lane * seg + step * CHUNKS
            adj = fma(lam, adj, cload(adj_ref, at, CHUNKS))
            cstore(adj_ref, at, adj)
        leaving.append(copies.start(adj_ref.at[rows], adj_hbm.at[rows]))
        state = None
        for chunk in reversed(range(CHUNKS)):
            here = adj[0][chunk : chunk + 1], adj[1][chunk : chunk + 1]
            state = here if state is None else fma(lam_span, state, here)
            state = kept(keep_ref, lane * CHUNKS + chunk, state)
        cstore(back_ref, lane, state)
    g_d_ref[...] = total
    leaving.append(copies.start(carry_ref, carry_hbm))
    w_send_ref[...] = half_tn(gelu_ref[...], pre_ref[...], 1)
    wait(leaving)


def own_kernel(gelu_ref, pre_ref, states_ref, low_ref, c_go_hbm, w_go_ref, c_send_ref, c_go_ref, sems):
    put_halves(dot_tn(states_ref[...], low_ref[...]), c_go_ref, c_send_ref)
    copy = pltpu.make_async_copy(c_go_ref, c_go_hbm, sems.at[0])
    copy.start()
    w_go_ref[...] = half_tn(gelu_ref[...], pre_ref[...], 0)
    copy.wait()


def states_kernel(
    c_go_hbm, h_hbm, adj_hbm, normed_hbm, carry_ref, b_ref, gamma_ref, d_ref, leave_ref, pow_ref, keep_ref, g_d_ref,
    c_got_ref,
    low_hbm, go_ref, send_ref, c_ref, h_ref, adj_ref, normed_ref, low_ref, after_ref, small_ref, sems,
):
    copies = Copies(sems)
    h_here = copies.lanes(leave_ref.shape[0], (adj_hbm, adj_ref), (h_hbm, h_ref))
    normed_here = copies.start(normed_hbm, normed_ref)
    c_here = copies.start(c_go_hbm, c_ref)
    leaving = []
    lanes = leave_ref.shape[0]
    seg = normed_ref.shape[0] // lanes
    span = seg // CHUNKS
    back = conj(cload(pow_ref, span - 1))
    factor = jnp.exp(gamma_ref[...])
    sums = None
    for lane in range(lanes):
        first = lane * seg
        state = cload(leave_ref, lane)
        wait(h_here[lane])
        cstore(after_ref, CHUNKS - 1, state)
        for chunk in reversed(range(1, CHUNKS)):
            state = fma(back, state, cload(adj_ref, first + chunk))
            state = kept(keep_ref, lane * CHUNKS + chunk, state)
            cstore(after_ref, chunk - 1, state)
        after = cload(after_ref, 0, CHUNKS)
        before = cload(carry_ref, lane * CHUNKS, CHUNKS)
        for step in range(span):
            at = first + step * CHUNKS
            full = fma(conj(cload(pow_ref, span - 1 - step)), after, cload(adj_ref, at, CHUNKS))
            add = cmul(conj(before), full)
            sums = add if sums is None else cadd(sums, add)
            cstore(low_ref, at, ((full[0] * factor).astype(BF16), (full[1] * factor).astype(BF16)))
            before = cload(h_ref, at, CHUNKS)
        rows = pl.ds(first, seg)
        leaving.append(copies.start(low_ref.at[rows], low_hbm.at[rows]))
    normed_here.wait()
    grad_b = dot_tn(normed_ref[...], low_ref[...])
    n = gamma_ref.shape[1]
    prod = grad_b * b_ref[...].astype(F32)
    small_ref[...] = jnp.zeros_like(small_ref)
    small_ref[0:1, :n] = jnp.sum(sums[0], axis=0, keepdims=True)
    small_ref[0:1, n:] = jnp.sum(sums[1], axis=0, keepdims=True)
    small_ref[1:2, :] = jnp.sum(prod, axis=0, keepdims=True)
    small_ref[8:9, :] = jnp.sum(prod.T, axis=0, keepdims=True) + d_ref[...] * g_d_ref[...]
    small_ref[9:10, :] = g_d_ref[...]
    put_halves(grad_b, go_ref.at[pl.ds(0, n)], send_ref.at[pl.ds(0, n)])
    put_halves(small_ref[...], go_ref.at[pl.ds(n, 8)], send_ref.at[pl.ds(n, 8)])
    c_here.wait()
    c_ref[...] += c_got_ref[...]
    wait(leaving)


def put_pieces(get, own_ref, send_refs):
    rows = own_ref.shape[0]
    mine = lax.axis_index("dp")
    for mask, ref in enumerate((own_ref, *send_refs)):
        ref[:rows, :] = get(pl.ds(pl.multiple_of((mine ^ mask) * rows, rows), rows))


def c_pieces_kernel(c_ref, own_ref, *send_refs):
    put_pieces(lambda at: c_ref[at, :], own_ref, send_refs)


def b_pieces_kernel(keep_ref, got_ref, small_ref, own_ref, *send_refs):
    n = own_ref.shape[0] * (len(send_refs) + 1)
    small = keep_ref[n:, :] + got_ref[n:, :]
    small_ref[...] = small
    put_pieces(lambda at: keep_ref[at, :] + got_ref[at, :], own_ref, send_refs)
    for ref in send_refs:
        ref[own_ref.shape[0] :, :] = small


def split_kernel(phase, keep_ref, got_ref, own_ref, send_ref):
    rows = own_ref.shape[0]
    mine = my_bit(phase)
    if rows % 8:
        total = keep_ref[...] + got_ref[...]
        own_ref[...] = jnp.where(mine == 0, total[:rows], total[rows:])
        send_ref[...] = jnp.where(mine == 0, total[rows:], total[:rows])
        return
    for ref, which in ((own_ref, mine), (send_ref, 1 - mine)):
        at = pl.ds(pl.multiple_of(which * rows, rows), rows)
        ref[...] = keep_ref[at, :] + got_ref[at, :]


def input_kernel(
    gain_hbm, b_hbm, d_hbm, xs_hbm, cts_hbm, low_hbm, mixed_hbm, out_hbm,
    in_hbm, block_hbm, gain_ref, b_ref, d_ref, xs_ref, cts_ref, low_ref, mixed_ref, out_ref,
    in_ref, block_ref, sems,
):
    lanes, seg, width = in_ref.shape
    copies = Copies(sems)
    params = [copies.start(a, b) for a, b in ((gain_hbm, gain_ref), (b_hbm, b_ref), (d_hbm, d_ref))]
    here = copies.lanes(
        lanes, (low_hbm, low_ref), (mixed_hbm, mixed_ref), (xs_hbm, xs_ref), (cts_hbm, cts_ref),
        (out_hbm, out_ref),
    )
    wait(params)
    leaving = []
    order_back = scan_order(seg, True)
    for lane in range(lanes):
        rows = pl.ds(lane * seg, seg)
        wait(here[lane])
        grad_normed = dot_nt(low_ref[rows, :], b_ref[...]) + mixed_ref[rows, :] * d_ref[...]
        xhat, scale = norm_stats(xs_ref[rows, :].astype(F32))
        dxhat = grad_normed * gain_ref[...]
        one = jnp.mean(dxhat, axis=-1, keepdims=True)
        two = jnp.mean(dxhat * xhat, axis=-1, keepdims=True)
        grad = (cts_ref[rows, :].astype(F32) + (dxhat - one - xhat * two) * scale).astype(BF16)
        in_ref[lane] = dot_nn(order_back, grad).astype(BF16)
        leaving.append(copies.start(in_ref.at[lane], in_hbm.at[lane]))
        block_ref[lane] = dot_nn(order_back, out_ref[rows, :]).astype(BF16)
        leaving.append(copies.start(block_ref.at[lane], block_hbm.at[lane]))
    wait(leaving)


def finish_kernel(
    nu_hbm, th_hbm, gain_hbm, small_ref, pow_ref, gain_out, gamma_out, nu_out, th_out, d_out,
    nu_ref, th_ref, gain_ref, sems,
):
    n = nu_ref.shape[1]
    copies = Copies(sems)
    for copy in [copies.start(a, b) for a, b in ((nu_hbm, nu_ref), (th_hbm, th_ref), (gain_hbm, gain_ref))]:
        copy.wait()
    lam = cload(pow_ref, 0)
    p, q = small_ref[0:1, :n], small_ref[0:1, n:]
    nu_out[...] = -jnp.exp(nu_ref[...]) * (p * lam[0] + q * lam[1])
    th_out[...] = -jnp.exp(th_ref[...]) * (p * lam[1] - q * lam[0])
    gamma_out[...] = small_ref[1:2, :n] + small_ref[1:2, n:]
    gain_out[...] = small_ref[8:9, :] / gain_ref[...]
    d_out[...] = small_ref[9:10, :]


def swap(value, axis, bit):
    count = lax.axis_size(axis)
    return lax.ppermute(value, axis, [(i, i ^ (1 << bit)) for i in range(count)])


def entering(pair, backward, beside=None):
    lanes, n = pair.shape[0] // 2, pair.shape[1] // 2

    def mul(x, y):
        return jnp.concatenate(
            [x[:, :n] * y[:, :n] - x[:, n:] * y[:, n:], x[:, :n] * y[:, n:] + x[:, n:] * y[:, :n]], 1
        )

    def join(early, late):
        return late[0] + mul(late[1], early[0]), mul(late[1], early[1])

    count, mine = lax.axis_size("seq"), lax.axis_index("seq")
    one = jnp.concatenate([jnp.ones_like(pair[:lanes, :n]), jnp.zeros_like(pair[:lanes, n:])], 1)
    before = jnp.zeros_like(one), one
    bit = 0
    while 1 << bit < count:
        size = 2 if bit == 0 else min(4, count >> bit)
        if beside is not None and bit == (1 if not backward else 0):
            pair, beside = tie(pair, beside)
        parts = [pair] + [
            lax.ppermute(pair, "seq", [(i, i ^ (mask << bit)) for i in range(count)])
            for mask in reversed(range(1, size))
        ][::-1]
        place = mine // (1 << bit) % size ^ (size - 1 if backward else 0)
        ordered = []
        for k in range(size):
            part = parts[0]
            for mask in range(1, size):
                part = jnp.where(place ^ k == mask, parts[mask], part)
            ordered.append((part[:lanes], part[lanes:]))
        sofar = None
        for k, item in enumerate(ordered):
            if k:
                joined = join(sofar, before)
                before = tuple(jnp.where(place == k, new, old) for new, old in zip(joined, before))
            sofar = item if sofar is None else join(sofar, item)
        pair = jnp.concatenate(sofar, 0)
        bit += size.bit_length() - 1
    return before[0] if beside is None else (before[0], beside)


def bits(axis, first=0):
    return [(axis, bit) for bit in range(first, lax.axis_size(axis).bit_length() - 1)]


def phases(first=False):
    dp, far = bits("dp"), bits("seq", 1)
    if first:
        return [dp + far, dp[::-1] + far]
    return [dp + far, dp[::-1] + far]


def hop(value, phase):
    orders, count = phases(phase < 0), lax.axis_size("seq")
    phase = phase if phase >= 0 else -1 - phase
    pairs = []
    for device in range(lax.axis_size("dp") * count):
        axis, bit = orders[device % 2][phase]
        pairs.append((device, device ^ ((1 << bit) * (count if axis == "dp" else 1))))
    return lax.ppermute(value, ("dp", "seq"), pairs)


def my_bit(phase):
    place = phase if phase >= 0 else -1 - phase
    one, two = (lax.axis_index(axis) // (1 << bit) % 2 for axis, bit in (o[place] for o in phases(phase < 0)))
    return jnp.where(lax.axis_index("seq") % 2 == 0, one, two)


def piece(value, which, count):
    rows = value.shape[1] // count
    return lax.dynamic_slice(value, (0, which * rows, 0), (value.shape[0], rows, value.shape[2]))


def pack(value, extra):
    if extra is None:
        return value
    return jnp.concatenate([value.reshape(-1, value.shape[2]), extra], 0)


def unpack(sent, value, extra):
    if extra is None:
        return sent, None
    rows = value.shape[0] * value.shape[1]
    return sent[:rows].reshape(value.shape), sent[rows:]


def tree_sum(values):
    while len(values) > 1:
        values = [a + b for a, b in zip(values[::2], values[1::2])]
    return values[0]


def scatter(value, phase, extra=None):
    mine = my_bit(phase)
    send, keep = piece(value, 1 - mine, 2), piece(value, mine, 2)
    got, more = unpack(hop(pack(send, extra), phase), send, extra)
    return keep + got, None if extra is None else extra + more


def double(value, phase, extra=None):
    got, more = unpack(hop(pack(value, extra), phase), value, extra)
    return value + got, None if extra is None else extra + more


def gather(value, phase):
    got = hop(value, phase)
    return join_rows([value, got], my_bit(phase))


def join_rows(parts, mine):
    count = len(parts)
    if count == 1:
        return parts[0]
    half = count // 2
    low = join_rows(parts[:half], mine % half)
    high = join_rows(parts[half:], mine % half)
    first = mine // half == 0
    return jnp.where(first, jnp.concatenate([low, high], 1), jnp.concatenate([high, low], 1))


def across(value, mask):
    return lax.ppermute(value, "dp", [(i, i ^ mask) for i in range(lax.axis_size("dp"))])


def sum_dp(own, sends, extra):
    parts, extras = [own], [extra]
    for mask, send in enumerate(sends):
        got, more = unpack(across(send, mask + 1), own, extra)
        parts.append(got)
        extras.append(more)
    return tree_sum(parts), None if extra is None else tree_sum(extras)


def gather_dp(value):
    count, mine = lax.axis_size("dp"), lax.axis_index("dp")
    parts = [value]
    for mask in reversed(range(1, count)):
        parts.insert(1, across(value, mask))
    return join_rows(parts, mine)


def only(step):
    return lambda value, extra=None: (step(value), extra)


def tie(*values):
    return lax.optimization_barrier(values)


def after(value, *others):
    for other in others:
        value = value + jnp.minimum(jnp.abs(other[(0,) * other.ndim]), 0.0)
    return value


def assemble_kernel(mine, other, *refs):
    whole, sems = refs[:-1], refs[-1]
    copies = Copies(sems)
    rows = mine.shape[0]
    first = pl.multiple_of(lax.rem(lax.axis_index("seq"), 2) * rows, rows)
    column = 0
    for out in whole:
        columns = pl.ds(column, out.shape[1])
        copies.start(mine.at[:, columns], out.at[pl.ds(first, rows)])
        copies.start(other.at[:, columns], out.at[pl.ds(pl.multiple_of(rows - first, rows), rows)])
        column += out.shape[1]
    wait(copies.all)


def on_device(
    block_in, cotangent, bucket_id, assignment, norm_gain, b_proj, gamma_log, nu_log, theta_log,
    c_proj, d_skip, glu_weight,
):
    _, lanes, seg, width = block_in.shape
    n = nu_log.shape[0]
    two = 2 * n
    tokens = lanes * seg
    span = seg // CHUNKS
    short = seg * lax.axis_size("seq") // bucket_id.shape[2]
    gain, gamma, nu, theta, skip = (
        v.reshape(1, -1) for v in (norm_gain, gamma_log, nu_log, theta_log, d_skip)
    )
    hbm, vmem = pl.BlockSpec(memory_space=pltpu.HBM), pl.BlockSpec(memory_space=pltpu.VMEM)

    def call(kernel, name, micros, outs, far, near, fetched=None, scratch=(), sems=0, far_outs=0, limit=4, pin=False, wait_for=()):
        fetched = far if fetched is None else fetched
        far = [pltpu.with_memory_space_constraint(v, pltpu.HBM) for v in far]
        if pin:
            near = [pltpu.with_memory_space_constraint(v, pltpu.VMEM) for v in near]
        shapes = [
            pltpu.HBM(shape, kind) if k < far_outs else jax.ShapeDtypeStruct(shape, kind)
            for k, (shape, kind) in enumerate(outs)
        ]
        room = [(pltpu.SMEM if v.dtype == jnp.int32 else pltpu.VMEM)(v.shape, v.dtype) for v in fetched]
        count, extra = len(far) + len(near), len(wait_for)

        def body(*refs):
            kernel(*refs[:count], *refs[count + extra :])

        return pl.pallas_call(
            body,
            in_specs=[hbm] * len(far) + [vmem] * len(near) + [pl.BlockSpec(memory_space=pl.ANY)] * extra,
            out_specs=[hbm] * far_outs + [vmem] * (len(outs) - far_outs),
            out_shape=shapes,
            scratch_shapes=room
            + [pltpu.VMEM(shape, kind) for shape, kind in scratch]
            + ([pltpu.SemaphoreType.DMA((sems,))] if sems else []),
            compiler_params=pltpu.CompilerParams(vmem_limit_bytes=limit * 1024 * 1024),
            cost_estimate=cost(micros),
            name=name,
        )(*far, *near, *wait_for)

    low_rows, full_rows = ((tokens, width), BF16), ((tokens, two), F32)
    lane_rows = ((lanes, seg, width), BF16)
    xs, normed, loc, pair, powers, keep = call(
        functools.partial(first_kernel, short), "forward_local", 4,
        [
            low_rows, low_rows, full_rows, ((2 * lanes, two), F32), ((span, two), F32),
            ((lanes * CHUNKS, two), F32),
        ],
        [bucket_id[0], assignment, block_in[0], gain, b_proj, gamma, nu, theta], [],
        scratch=[low_rows, low_rows, full_rows], sems=4 * lanes + 7, far_outs=3, limit=12,
    )
    enter, cotangent_later = entering(pair, False, cotangent[0])
    (cts,) = call(
        order_kernel, "cotangent_order", 2, [low_rows], [cotangent_later], [],
        scratch=[low_rows], sems=2 * lanes, far_outs=1, limit=8,
    )

    chunk_rows, half_rows = ((lanes * CHUNKS, two), F32), ((n, width), F32)
    out, h, grad_mixed, adj, carry, back_total, grad_d, w_send, states, gelu, pre, low = call(
        block_kernel, "block", 10,
        [
            low_rows, full_rows, full_rows, full_rows, chunk_rows, ((lanes, two), F32), ((1, width), F32),
            ((n, 2 * width), F32), low_rows, low_rows, ((tokens, 2 * width), BF16), low_rows,
        ],
        [glu_weight, c_proj, skip, xs, normed, loc, cts], [enter, powers, keep], fetched=(),
        scratch=[
            chunk_rows, ((width, 2 * width), BF16), ((two, width), BF16), ((1, width), F32),
            low_rows, low_rows, full_rows, low_rows, low_rows, full_rows, full_rows, full_rows,
        ],
        sems=4 * lanes + 12, far_outs=5, limit=30,
    )
    c_keep, w_keep, c_send = call(
        own_kernel, "own_grads", 2, [half_rows, ((n, 2 * width), F32), half_rows],
        [], [gelu, pre, states, low], scratch=[half_rows], sems=1, far_outs=1, limit=8,
    )

    decay = pair[lanes:]
    back_pair = jnp.concatenate(
        [back_total, jnp.concatenate([decay[:, :n], -decay[:, n:]], 1)], 0
    )
    near, last = len(bits("dp")), len(phases()[0]) - 1
    c_got = swap(c_send, "seq", 0)

    def split(keep, got, phase):
        half = ((keep.shape[0] // 2, keep.shape[1]), F32)
        return call(
            functools.partial(split_kernel, phase), "split_sum", 0.5, [half, half], [], [keep, got], pin=True
        )

    own, send = split(w_keep, swap(w_send, "seq", 0), -1)
    leave, own = entering(back_pair, True, own)
    owns = [own]
    for phase in range(1, last):
        own, send = split(own, hop(send, -phase), -1 - phase)
        owns.append(own)
    w = (own + hop(send, -last))[None]
    w_steps = [functools.partial(double, phase=-1 - last)]
    w_steps += [only(functools.partial(gather, phase=-1 - p)) for p in reversed(range(last))]
    for step in w_steps:
        w, _ = step(w)

    back_low, b_keep, b_send, c = call(
        states_kernel, "adjoint_states", 3,
        [low_rows, ((n + 8, two), F32), ((n + 8, two), F32), half_rows],
        [c_keep, h, adj, normed], [carry, b_proj, gamma, skip, leave, powers, keep, grad_d, c_got], fetched=(),
        scratch=[full_rows, full_rows, low_rows, low_rows, ((CHUNKS, two), F32), ((16, two), F32)],
        sems=3 * lanes + 2, far_outs=1, limit=14, wait_for=[owns[1]],
    )

    def back_input(back_low):
        return call(
            input_kernel, "back_input", 4, [lane_rows, lane_rows],
            [gain, b_proj, skip, xs, cts, back_low, grad_mixed, out], [], wait_for=[cb, finished[0], w],
            scratch=[lane_rows, lane_rows], sems=7 * lanes + 3, far_outs=2, limit=12,
        )

    groups = lax.axis_size("dp")
    cut = n // groups
    piece_rows = ((cut, width), F32)
    c_own, *c_sends = call(c_pieces_kernel, "c_pieces", 0.5, [piece_rows] * groups, [], [c])
    c, _ = sum_dp(c_own[None], [v[None] for v in c_sends], None)
    small, b_own, *b_sends = call(
        b_pieces_kernel, "b_pieces", 0.5,
        [((8, two), F32), piece_rows] + [((cut + 8, width), F32)] * (groups - 1),
        [], [b_keep, swap(b_send, "seq", 0)], wait_for=[owns[2]],
    )
    b, small = sum_dp(b_own[None], b_sends, small)
    cb = jnp.concatenate([c, b], 0)

    steps = [functools.partial(scatter, phase=p) for p in range(near, last)]
    steps += [functools.partial(double, phase=last)]
    steps += [only(functools.partial(gather, phase=p)) for p in reversed(range(near, last))]
    for step in steps:
        cb, small = step(cb, extra=small)
    got = swap(small, "seq", 0)
    small = join_rows([small[None], got[None]], lax.axis_index("seq") % 2)[0]
    finished = call(
        finish_kernel, "finish", 1, [((1, v), F32) for v in (width, n, n, n, width)],
        [nu, theta, gain], [small, powers], sems=3,
    )
    grad_in, block_out = back_input(back_low)
    cb, w = tie(cb, w)
    cb = gather_dp(cb)
    cb, grad_in, block_out = tie(cb, grad_in, block_out)
    w, cb = w[0], jnp.concatenate([cb[0], cb[1]], 1)

    grad_gain, grad_gamma, grad_nu, grad_theta, grad_d = finished

    def assemble(mine, widths, wait_for):
        return call(
            assemble_kernel, "assemble", 2, [((2 * mine.shape[0], v), F32) for v in widths],
            [], [mine, swap(mine, "seq", 0)], sems=2 * len(widths), far_outs=len(widths), pin=True, wait_for=wait_for,
        )

    (grad_w,) = assemble(w, [2 * width], [grad_in])
    grad_c, grad_b = assemble(cb, [width, two], [])
    return (
        block_out[None], grad_in[None], grad_gain[0], grad_b, grad_gamma[0], grad_nu[0], grad_theta[0],
        grad_c, grad_d[0], grad_w,
    )


def solution(mesh):
    rows = P("dp", None, "seq", None)
    in_specs = (rows, rows, P("dp", None, None), P("dp", None)) + (P(),) * 8
    out_specs = (rows, rows) + (P(),) * 8
    return jax.shard_map(
        on_device, mesh=mesh, in_specs=in_specs, out_specs=out_specs, check_vma=False
    )
```

```python
import functools

import jax
import jax.numpy as jnp
from jax import lax
from jax.experimental import pallas as pl
from jax.experimental.pallas import tpu as pltpu
from jax.sharding import PartitionSpec as P

EPS = 1e-05
CHUNKS = 8
GELU_A = 0.044715
GELU_K = 0.7978845608028654
F32 = jnp.float32
BF16 = jnp.bfloat16


def dot_nt(left, right):
    return lax.dot_general(left, right, (((1,), (1,)), ((), ())), preferred_element_type=F32)


def dot_tn(left, right):
    return lax.dot_general(left, right, (((0,), (0,)), ((), ())), preferred_element_type=F32)


def dot_nn(left, right):
    return jnp.dot(left, right, preferred_element_type=F32)


def cmul(x, y):
    return x[0] * y[0] - x[1] * y[1], x[0] * y[1] + x[1] * y[0]


def cadd(x, y):
    return x[0] + y[0], x[1] + y[1]


def fma(a, x, y):
    return (y[0] - a[1] * x[1]) + a[0] * x[0], (y[1] + a[1] * x[0]) + a[0] * x[1]


def conj(x):
    return x[0], -x[1]


def cload(ref, first, count=1):
    n = ref.shape[-1] // 2
    return ref[first : first + count, :n], ref[first : first + count, n:]


def cstore(ref, first, value):
    n = ref.shape[-1] // 2
    rows = value[0].shape[0]
    ref[first : first + rows, :n], ref[first : first + rows, n:] = value


def kept(ref, row, value):
    keep = cload(ref, row)
    return value[0] * keep[0], value[1] * keep[1]


def scan_order(seg, back=False):
    row = lax.broadcasted_iota(jnp.int32, (seg, seg), 0)
    column = lax.broadcasted_iota(jnp.int32, (seg, seg), 1)
    if back:
        row, column = column, row
    span = seg // CHUNKS
    hit = (row % CHUNKS == column // span) & (row // CHUNKS == column % span)
    return jnp.where(hit, 1.0, 0.0).astype(BF16)


def fill_keeps(bucket, assign, keep_ref, lanes, seg, short):
    own = lax.axis_index("seq")
    for lane in range(lanes):
        pattern = assign[0, lane]
        for chunk in range(CHUNKS):
            token = own * seg + chunk * (seg // CHUNKS)
            here = bucket[pattern, lax.div(token, short)]
            span = jnp.where(here == 0, short, jnp.where(here == 1, 4 * short, 16 * short))
            keep = jnp.where(lax.rem(token, span) == 0, 0.0, 1.0).astype(F32)
            row = lane * CHUNKS + chunk
            keep_ref[row : row + 1, :] = jnp.full((1, keep_ref.shape[1]), keep)


def norm_stats(rows):
    mean = jnp.mean(rows, axis=-1, keepdims=True)
    centred = rows - mean
    var = jnp.mean(centred * centred, axis=-1, keepdims=True)
    scale = lax.rsqrt(var + EPS)
    return centred * scale, scale


def cost(micros):
    return pl.CostEstimate(flops=int(micros * 1.1e9), bytes_accessed=int(micros * 3e6), transcendentals=0)


def put_halves(value, keep, send):
    rows = value.shape[0] // 2
    first = lax.rem(lax.axis_index("seq"), 2) == 0
    top, bottom = value[:rows], value[rows:]
    keep[...] = jnp.where(first, top, bottom)
    send[...] = jnp.where(first, bottom, top)


def half_tn(left, right, other):
    columns = left.shape[1] // 2
    first = lax.rem(lax.axis_index("seq"), 2) == other
    return dot_tn(jnp.where(first, left[:, :columns], left[:, columns:]), right)


class Copies:
    def __init__(self, sems):
        self.sems, self.all = sems, []

    def start(self, source, target):
        copy = pltpu.make_async_copy(source, target, self.sems.at[len(self.all)])
        copy.start()
        self.all.append(copy)
        return copy

    def lanes(self, lanes, *pairs):
        return [
            [self.start(lane_of(source, lane, lanes), lane_of(target, lane, lanes)) for source, target in pairs]
            for lane in range(lanes)
        ]


def lane_of(ref, lane, lanes):
    if len(ref.shape) == 3:
        return ref.at[lane]
    rows = ref.shape[0] // lanes
    return ref.at[pl.ds(lane * rows, rows)]


def wait(copies):
    for copy in copies:
        copy.wait()


def first_kernel(
    short, bucket_hbm, assign_hbm, x_hbm, gain_hbm, b_hbm, gamma_hbm, nu_hbm, th_hbm,
    xs_hbm, normed_hbm, loc_hbm, pair_ref, pow_ref, keep_ref,
    bucket, assign, x_ref, gain_ref, b_ref, gamma_ref, nu_ref, th_ref, xs_ref, normed_ref, loc_ref, sems,
):
    lanes, seg, width = x_ref.shape
    span = seg // CHUNKS
    copies = Copies(sems)
    x_here = copies.lanes(lanes, (x_hbm, x_ref))
    nu_here, th_here = copies.start(nu_hbm, nu_ref), copies.start(th_hbm, th_ref)
    gain_here, gamma_here = copies.start(gain_hbm, gain_ref), copies.start(gamma_hbm, gamma_ref)
    b_here = copies.start(b_hbm, b_ref)
    tables = copies.start(bucket_hbm, bucket), copies.start(assign_hbm, assign)
    leaving = []

    order = scan_order(seg)
    nu_here.wait(), th_here.wait()
    modulus = jnp.exp(-jnp.exp(nu_ref[...]))
    phase = jnp.exp(th_ref[...])
    cstore(pow_ref, 0, (modulus * jnp.cos(phase), modulus * jnp.sin(phase)))
    size = 1
    while size < span:
        cstore(pow_ref, size, cmul(cload(pow_ref, 0, size), cload(pow_ref, size - 1)))
        size *= 2

    gain_here.wait(), gamma_here.wait()
    lam = cload(pow_ref, 0)
    lam_span = cload(pow_ref, span - 1)
    ends = []
    factor = jnp.exp(gamma_ref[...])
    factor = jnp.concatenate([factor, factor], 1)
    for lane in range(lanes):
        rows = pl.ds(lane * seg, seg)
        wait(x_here[lane])
        x = dot_nn(order, x_ref[lane])
        xs_ref[rows, :] = x.astype(BF16)
        xhat, _ = norm_stats(x)
        low = (xhat * gain_ref[...]).astype(BF16)
        normed_ref[rows, :] = low
        if lane == 0:
            b_here.wait()
        loc_ref[rows, :] = dot_nn(low, b_ref[...]) * factor
        for source, target in ((xs_ref, xs_hbm), (normed_ref, normed_hbm)):
            leaving.append(copies.start(source.at[rows], target.at[rows]))
        h = cload(loc_ref, lane * seg, CHUNKS)
        for step in range(1, span):
            at = lane * seg + step * CHUNKS
            h = fma(lam, h, cload(loc_ref, at, CHUNKS))
            cstore(loc_ref, at, h)
        leaving.append(copies.start(loc_ref.at[rows], loc_hbm.at[rows]))
        ends.append(h)

    wait(tables)
    fill_keeps(bucket, assign, keep_ref, lanes, seg, short)
    for lane, h in enumerate(ends):
        state = h[0][0:1], h[1][0:1]
        decay = kept(keep_ref, lane * CHUNKS, lam_span)
        for chunk in range(1, CHUNKS):
            step = kept(keep_ref, lane * CHUNKS + chunk, lam_span)
            state = fma(step, state, (h[0][chunk : chunk + 1], h[1][chunk : chunk + 1]))
            decay = cmul(step, decay)
        cstore(pair_ref, lane, state)
        cstore(pair_ref, lanes + lane, decay)
    wait(leaving)


def order_kernel(ct_hbm, cts_hbm, ct_ref, cts_ref, sems):
    lanes, seg, _ = ct_ref.shape
    copies = Copies(sems)
    here = copies.lanes(lanes, (ct_hbm, ct_ref))
    order = scan_order(seg)
    leaving = []
    for lane in range(lanes):
        rows = pl.ds(lane * seg, seg)
        wait(here[lane])
        cts_ref[rows, :] = dot_nn(order, ct_ref[lane]).astype(BF16)
        leaving.append(copies.start(cts_ref.at[rows], cts_hbm.at[rows]))
    wait(leaving)


def block_kernel(
    w_hbm, c_hbm, d_hbm, xs_hbm, normed_hbm, loc_hbm, cts_hbm, enter_ref, pow_ref, keep_ref,
    out_hbm, h_hbm, mixed_hbm, adj_hbm, carry_hbm, back_ref, g_d_ref, w_send_ref,
    states_ref, gelu_ref, pre_ref, low_ref, carry_ref, w_ref, c_ref, d_ref, xs_ref, normed_ref, h_ref, cts_ref,
    out_ref, slope_ref, mixed_ref, adj_ref, sems,
):
    lanes, width = enter_ref.shape[0], d_ref.shape[1]
    seg = h_ref.shape[0] // lanes
    span = seg // CHUNKS
    copies = Copies(sems)
    one, rest = pl.ds(0, seg), pl.ds(seg, (lanes - 1) * seg)
    arrays = (loc_hbm, h_ref), (normed_hbm, normed_ref), (xs_hbm, xs_ref), (cts_hbm, cts_ref)
    loc_here = copies.start(loc_hbm.at[one], h_ref.at[one])
    c_here, d_here = copies.start(c_hbm, c_ref), copies.start(d_hbm, d_ref)
    normed_here = copies.start(normed_hbm.at[one], normed_ref.at[one])
    w_here = copies.start(w_hbm, w_ref)
    late_here = [copies.start(a.at[one], b.at[one]) for a, b in arrays[2:]]
    rest_here = [copies.start(a.at[rest], b.at[rest]) for a, b in arrays]
    leaving = []
    lam_span = cload(pow_ref, span - 1)
    for lane in range(lanes):
        first = lane * seg
        rows = pl.ds(first, seg)
        if lane == 0:
            loc_here.wait()
        elif lane == 1:
            wait(rest_here)
        last = first + (span - 1) * CHUNKS
        state = kept(keep_ref, lane * CHUNKS, cload(enter_ref, lane))
        cstore(carry_ref, lane * CHUNKS, state)
        for chunk in range(1, CHUNKS):
            state = fma(lam_span, state, cload(h_ref, last + chunk - 1))
            state = kept(keep_ref, lane * CHUNKS + chunk, state)
            cstore(carry_ref, lane * CHUNKS + chunk, state)
        carry = cload(carry_ref, lane * CHUNKS, CHUNKS)
        for step in range(span):
            at = first + step * CHUNKS
            cstore(h_ref, at, fma(cload(pow_ref, step), carry, cload(h_ref, at, CHUNKS)))
        leaving.append(copies.start(h_ref.at[rows], h_hbm.at[rows]))

        states = h_ref[rows, :].astype(BF16)
        states_ref[rows, :] = states
        if lane == 0:
            wait([normed_here, c_here, d_here])
        mixed = dot_nn(states, c_ref[...]) + d_ref[...] * normed_ref[rows, :].astype(F32)
        square = mixed * mixed
        tanh = jnp.tanh(GELU_K * mixed * (1.0 + GELU_A * square))
        half_up = 0.5 * (1.0 + tanh)
        gelu = (mixed * half_up).astype(BF16)
        gelu_ref[rows, :] = gelu
        slope_ref[rows, :] = half_up + 0.5 * GELU_K * mixed * (1.0 - tanh * tanh) * (
            1.0 + 3.0 * GELU_A * square
        )
        if lane == 0:
            w_here.wait()
        pre = dot_nn(gelu, w_ref[...])
        value = pre[:, :width]
        sig = jax.nn.sigmoid(pre[:, width:])
        gated = value * sig
        if lane == 0:
            wait(late_here)
        out_ref[rows, :] = (xs_ref[rows, :].astype(F32) + gated).astype(BF16)
        leaving.append(copies.start(out_ref.at[rows], out_hbm.at[rows]))
        grad_value = cts_ref[rows, :].astype(F32) * sig
        pre_ref[rows, :width] = grad_value.astype(BF16)
        pre_ref[rows, width:] = (grad_value * (value - gated)).astype(BF16)

    lam, lam_span = conj(cload(pow_ref, 0)), conj(lam_span)
    total = None
    for lane in range(lanes):
        rows = pl.ds(lane * seg, seg)
        grad_mixed = dot_nt(pre_ref[rows, :], w_ref[...]) * slope_ref[rows, :]
        mixed_ref[rows, :] = grad_mixed
        leaving.append(copies.start(mixed_ref.at[rows], mixed_hbm.at[rows]))
        add = jnp.sum(grad_mixed * normed_ref[rows, :].astype(F32), axis=0, keepdims=True)
        total = add if total is None else total + add
        low = grad_mixed.astype(BF16)
        low_ref[rows, :] = low
        adj_ref[rows, :] = dot_nt(low, c_ref[...])
        adj = cload(adj_ref, (lane + 1) * seg - CHUNKS, CHUNKS)
        for step in reversed(range(span - 1)):
            at = lane * seg + step * CHUNKS
            adj = fma(lam, adj, cload(adj_ref, at, CHUNKS))
            cstore(adj_ref, at, adj)
        leaving.append(copies.start(adj_ref.at[rows], adj_hbm.at[rows]))
        state = None
        for chunk in reversed(range(CHUNKS)):
            here = adj[0][chunk : chunk + 1], adj[1][chunk : chunk + 1]
            state = here if state is None else fma(lam_span, state, here)
            state = kept(keep_ref, lane * CHUNKS + chunk, state)
        cstore(back_ref, lane, state)
    g_d_ref[...] = total
    leaving.append(copies.start(carry_ref, carry_hbm))
    w_send_ref[...] = half_tn(gelu_ref[...], pre_ref[...], 1)
    wait(leaving)


def own_kernel(gelu_ref, pre_ref, states_ref, low_ref, c_go_hbm, w_go_ref, c_send_ref, c_go_ref, sems):
    put_halves(dot_tn(states_ref[...], low_ref[...]), c_go_ref, c_send_ref)
    copy = pltpu.make_async_copy(c_go_ref, c_go_hbm, sems.at[0])
    copy.start()
    w_go_ref[...] = half_tn(gelu_ref[...], pre_ref[...], 0)
    copy.wait()


def states_kernel(
    c_go_hbm, h_hbm, adj_hbm, normed_hbm, carry_ref, b_ref, gamma_ref, d_ref, leave_ref, pow_ref, keep_ref, g_d_ref,
    c_got_ref,
    low_hbm, go_ref, send_ref, c_ref, h_ref, adj_ref, normed_ref, low_ref, after_ref, small_ref, sems,
):
    copies = Copies(sems)
    h_here = copies.lanes(leave_ref.shape[0], (adj_hbm, adj_ref), (h_hbm, h_ref))
    normed_here = copies.start(normed_hbm, normed_ref)
    c_here = copies.start(c_go_hbm, c_ref)
    leaving = []
    lanes = leave_ref.shape[0]
    seg = normed_ref.shape[0] // lanes
    span = seg // CHUNKS
    back = conj(cload(pow_ref, span - 1))
    factor = jnp.exp(gamma_ref[...])
    sums = None
    for lane in range(lanes):
        first = lane * seg
        state = cload(leave_ref, lane)
        wait(h_here[lane])
        cstore(after_ref, CHUNKS - 1, state)
        for chunk in reversed(range(1, CHUNKS)):
            state = fma(back, state, cload(adj_ref, first + chunk))
            state = kept(keep_ref, lane * CHUNKS + chunk, state)
            cstore(after_ref, chunk - 1, state)
        after = cload(after_ref, 0, CHUNKS)
        before = cload(carry_ref, lane * CHUNKS, CHUNKS)
        for step in range(span):
            at = first + step * CHUNKS
            full = fma(conj(cload(pow_ref, span - 1 - step)), after, cload(adj_ref, at, CHUNKS))
            add = cmul(conj(before), full)
            sums = add if sums is None else cadd(sums, add)
            cstore(low_ref, at, ((full[0] * factor).astype(BF16), (full[1] * factor).astype(BF16)))
            before = cload(h_ref, at, CHUNKS)
        rows = pl.ds(first, seg)
        leaving.append(copies.start(low_ref.at[rows], low_hbm.at[rows]))
    normed_here.wait()
    grad_b = dot_tn(normed_ref[...], low_ref[...])
    n = gamma_ref.shape[1]
    prod = grad_b * b_ref[...].astype(F32)
    small_ref[...] = jnp.zeros_like(small_ref)
    small_ref[0:1, :n] = jnp.sum(sums[0], axis=0, keepdims=True)
    small_ref[0:1, n:] = jnp.sum(sums[1], axis=0, keepdims=True)
    small_ref[1:2, :] = jnp.sum(prod, axis=0, keepdims=True)
    narrow = sum(prod[:, k : k + 128] for k in range(0, 2 * n, 128))
    small_ref[8:9, :] = jnp.sum(narrow.T, axis=0, keepdims=True) + d_ref[...] * g_d_ref[...]
    small_ref[9:10, :] = g_d_ref[...]
    put_halves(grad_b, go_ref.at[pl.ds(0, n)], send_ref.at[pl.ds(0, n)])
    put_halves(small_ref[...], go_ref.at[pl.ds(n, 8)], send_ref.at[pl.ds(n, 8)])
    c_here.wait()
    c_ref[...] += c_got_ref[...]
    wait(leaving)


def put_pieces(get, own_ref, send_refs):
    rows = own_ref.shape[0]
    mine = lax.axis_index("dp")
    for mask, ref in enumerate((own_ref, *send_refs)):
        ref[:rows, :] = get(pl.ds(pl.multiple_of((mine ^ mask) * rows, rows), rows))


def c_pieces_kernel(c_ref, own_ref, *send_refs):
    put_pieces(lambda at: c_ref[at, :], own_ref, send_refs)


def b_pieces_kernel(keep_ref, got_ref, small_ref, own_ref, *send_refs):
    n = own_ref.shape[0] * (len(send_refs) + 1)
    small = keep_ref[n:, :] + got_ref[n:, :]
    small_ref[...] = small
    put_pieces(lambda at: keep_ref[at, :] + got_ref[at, :], own_ref, send_refs)
    for ref in send_refs:
        ref[own_ref.shape[0] :, :] = small


def split_kernel(phase, keep_ref, got_ref, own_ref, send_ref):
    rows = own_ref.shape[0]
    mine = my_bit(phase)
    if rows % 8:
        total = keep_ref[...] + got_ref[...]
        own_ref[...] = jnp.where(mine == 0, total[:rows], total[rows:])
        send_ref[...] = jnp.where(mine == 0, total[rows:], total[:rows])
        return
    for ref, which in ((own_ref, mine), (send_ref, 1 - mine)):
        at = pl.ds(pl.multiple_of(which * rows, rows), rows)
        ref[...] = keep_ref[at, :] + got_ref[at, :]


def input_kernel(
    gain_hbm, b_hbm, d_hbm, xs_hbm, cts_hbm, low_hbm, mixed_hbm, out_hbm,
    in_hbm, block_hbm, gain_ref, b_ref, d_ref, xs_ref, cts_ref, low_ref, mixed_ref, out_ref,
    in_ref, block_ref, sems,
):
    lanes, seg, width = in_ref.shape
    copies = Copies(sems)
    params = [copies.start(a, b) for a, b in ((gain_hbm, gain_ref), (b_hbm, b_ref), (d_hbm, d_ref))]
    here = copies.lanes(
        lanes, (low_hbm, low_ref), (mixed_hbm, mixed_ref), (xs_hbm, xs_ref), (cts_hbm, cts_ref),
        (out_hbm, out_ref),
    )
    wait(params)
    leaving = []
    order_back = scan_order(seg, True)
    for lane in range(lanes):
        rows = pl.ds(lane * seg, seg)
        wait(here[lane])
        grad_normed = dot_nt(low_ref[rows, :], b_ref[...]) + mixed_ref[rows, :] * d_ref[...]
        xhat, scale = norm_stats(xs_ref[rows, :].astype(F32))
        dxhat = grad_normed * gain_ref[...]
        one = jnp.mean(dxhat, axis=-1, keepdims=True)
        two = jnp.mean(dxhat * xhat, axis=-1, keepdims=True)
        grad = (cts_ref[rows, :].astype(F32) + (dxhat - one - xhat * two) * scale).astype(BF16)
        in_ref[lane] = dot_nn(order_back, grad).astype(BF16)
        leaving.append(copies.start(in_ref.at[lane], in_hbm.at[lane]))
        block_ref[lane] = dot_nn(order_back, out_ref[rows, :]).astype(BF16)
        leaving.append(copies.start(block_ref.at[lane], block_hbm.at[lane]))
    wait(leaving)


def finish_kernel(
    nu_hbm, th_hbm, gain_hbm, small_ref, pow_ref, gain_out, gamma_out, nu_out, th_out, d_out,
    nu_ref, th_ref, gain_ref, sems,
):
    n = nu_ref.shape[1]
    copies = Copies(sems)
    for copy in [copies.start(a, b) for a, b in ((nu_hbm, nu_ref), (th_hbm, th_ref), (gain_hbm, gain_ref))]:
        copy.wait()
    lam = cload(pow_ref, 0)
    p, q = small_ref[0:1, :n], small_ref[0:1, n:]
    nu_out[...] = -jnp.exp(nu_ref[...]) * (p * lam[0] + q * lam[1])
    th_out[...] = -jnp.exp(th_ref[...]) * (p * lam[1] - q * lam[0])
    gamma_out[...] = small_ref[1:2, :n] + small_ref[1:2, n:]
    gain_out[...] = small_ref[8:9, :] / gain_ref[...]
    d_out[...] = small_ref[9:10, :]


def swap(value, axis, bit):
    count = lax.axis_size(axis)
    return lax.ppermute(value, axis, [(i, i ^ (1 << bit)) for i in range(count)])


def entering(pair, backward, beside=None):
    lanes, n = pair.shape[0] // 2, pair.shape[1] // 2

    def mul(x, y):
        return jnp.concatenate(
            [x[:, :n] * y[:, :n] - x[:, n:] * y[:, n:], x[:, :n] * y[:, n:] + x[:, n:] * y[:, :n]], 1
        )

    def join(early, late):
        return late[0] + mul(late[1], early[0]), mul(late[1], early[1])

    count, mine = lax.axis_size("seq"), lax.axis_index("seq")
    one = jnp.concatenate([jnp.ones_like(pair[:lanes, :n]), jnp.zeros_like(pair[:lanes, n:])], 1)
    before = jnp.zeros_like(one), one
    bit = 0
    while 1 << bit < count:
        size = 2 if bit == 0 else min(4, count >> bit)
        if beside is not None and bit == (1 if not backward else 0):
            pair, beside = tie(pair, beside)
        parts = [pair] + [
            lax.ppermute(pair, "seq", [(i, i ^ (mask << bit)) for i in range(count)])
            for mask in reversed(range(1, size))
        ][::-1]
        place = mine // (1 << bit) % size ^ (size - 1 if backward else 0)
        ordered = []
        for k in range(size):
            part = parts[0]
            for mask in range(1, size):
                part = jnp.where(place ^ k == mask, parts[mask], part)
            ordered.append((part[:lanes], part[lanes:]))
        sofar = None
        for k, item in enumerate(ordered):
            if k:
                joined = join(sofar, before)
                before = tuple(jnp.where(place == k, new, old) for new, old in zip(joined, before))
            sofar = item if sofar is None else join(sofar, item)
        pair = jnp.concatenate(sofar, 0)
        bit += size.bit_length() - 1
    return before[0] if beside is None else (before[0], beside)


def bits(axis, first=0):
    return [(axis, bit) for bit in range(first, lax.axis_size(axis).bit_length() - 1)]


def phases(first=False):
    dp, far = bits("dp"), bits("seq", 1)
    if first:
        return [dp + far, dp[::-1] + far]
    return [dp + far, dp[::-1] + far]


def hop(value, phase):
    orders, count = phases(phase < 0), lax.axis_size("seq")
    phase = phase if phase >= 0 else -1 - phase
    pairs = []
    for device in range(lax.axis_size("dp") * count):
        axis, bit = orders[device % 2][phase]
        pairs.append((device, device ^ ((1 << bit) * (count if axis == "dp" else 1))))
    return lax.ppermute(value, ("dp", "seq"), pairs)


def my_bit(phase):
    place = phase if phase >= 0 else -1 - phase
    one, two = (lax.axis_index(axis) // (1 << bit) % 2 for axis, bit in (o[place] for o in phases(phase < 0)))
    return jnp.where(lax.axis_index("seq") % 2 == 0, one, two)


def piece(value, which, count):
    rows = value.shape[1] // count
    return lax.dynamic_slice(value, (0, which * rows, 0), (value.shape[0], rows, value.shape[2]))


def pack(value, extra):
    if extra is None:
        return value
    return jnp.concatenate([value.reshape(-1, value.shape[2]), extra], 0)


def unpack(sent, value, extra):
    if extra is None:
        return sent, None
    rows = value.shape[0] * value.shape[1]
    return sent[:rows].reshape(value.shape), sent[rows:]


def tree_sum(values):
    while len(values) > 1:
        values = [a + b for a, b in zip(values[::2], values[1::2])]
    return values[0]


def scatter(value, phase, extra=None):
    mine = my_bit(phase)
    send, keep = piece(value, 1 - mine, 2), piece(value, mine, 2)
    got, more = unpack(hop(pack(send, extra), phase), send, extra)
    return keep + got, None if extra is None else extra + more


def double(value, phase, extra=None):
    got, more = unpack(hop(pack(value, extra), phase), value, extra)
    return value + got, None if extra is None else extra + more


def gather(value, phase):
    got = hop(value, phase)
    return join_rows([value, got], my_bit(phase))


def join_rows(parts, mine):
    count = len(parts)
    if count == 1:
        return parts[0]
    half = count // 2
    low = join_rows(parts[:half], mine % half)
    high = join_rows(parts[half:], mine % half)
    first = mine // half == 0
    return jnp.where(first, jnp.concatenate([low, high], 1), jnp.concatenate([high, low], 1))


def across(value, mask):
    return lax.ppermute(value, "dp", [(i, i ^ mask) for i in range(lax.axis_size("dp"))])


def sum_dp(own, sends, extra):
    parts, extras = [own], [extra]
    for mask, send in enumerate(sends):
        got, more = unpack(across(send, mask + 1), own, extra)
        parts.append(got)
        extras.append(more)
    return tree_sum(parts), None if extra is None else tree_sum(extras)


def gather_dp(value):
    count, mine = lax.axis_size("dp"), lax.axis_index("dp")
    parts = [value]
    for mask in reversed(range(1, count)):
        parts.insert(1, across(value, mask))
    return join_rows(parts, mine)


def only(step):
    return lambda value, extra=None: (step(value), extra)


def tie(*values):
    return lax.optimization_barrier(values)


def after(value, *others):
    for other in others:
        value = value + jnp.minimum(jnp.abs(other[(0,) * other.ndim]), 0.0)
    return value


def assemble_kernel(mine, other, *refs):
    whole, sems = refs[:-1], refs[-1]
    copies = Copies(sems)
    rows = mine.shape[0]
    first = pl.multiple_of(lax.rem(lax.axis_index("seq"), 2) * rows, rows)
    column = 0
    for out in whole:
        columns = pl.ds(column, out.shape[1])
        copies.start(mine.at[:, columns], out.at[pl.ds(first, rows)])
        copies.start(other.at[:, columns], out.at[pl.ds(pl.multiple_of(rows - first, rows), rows)])
        column += out.shape[1]
    wait(copies.all)


def on_device(
    block_in, cotangent, bucket_id, assignment, norm_gain, b_proj, gamma_log, nu_log, theta_log,
    c_proj, d_skip, glu_weight,
):
    _, lanes, seg, width = block_in.shape
    n = nu_log.shape[0]
    two = 2 * n
    tokens = lanes * seg
    span = seg // CHUNKS
    short = seg * lax.axis_size("seq") // bucket_id.shape[2]
    gain, gamma, nu, theta, skip = (
        v.reshape(1, -1) for v in (norm_gain, gamma_log, nu_log, theta_log, d_skip)
    )
    hbm, vmem = pl.BlockSpec(memory_space=pltpu.HBM), pl.BlockSpec(memory_space=pltpu.VMEM)

    def call(kernel, name, micros, outs, far, near, fetched=None, scratch=(), sems=0, far_outs=0, limit=4, pin=False, wait_for=()):
        fetched = far if fetched is None else fetched
        far = [pltpu.with_memory_space_constraint(v, pltpu.HBM) for v in far]
        if pin:
            near = [pltpu.with_memory_space_constraint(v, pltpu.VMEM) for v in near]
        shapes = [
            pltpu.HBM(shape, kind) if k < far_outs else jax.ShapeDtypeStruct(shape, kind)
            for k, (shape, kind) in enumerate(outs)
        ]
        room = [(pltpu.SMEM if v.dtype == jnp.int32 else pltpu.VMEM)(v.shape, v.dtype) for v in fetched]
        count, extra = len(far) + len(near), len(wait_for)

        def body(*refs):
            kernel(*refs[:count], *refs[count + extra :])

        return pl.pallas_call(
            body,
            in_specs=[hbm] * len(far) + [vmem] * len(near) + [pl.BlockSpec(memory_space=pl.ANY)] * extra,
            out_specs=[hbm] * far_outs + [vmem] * (len(outs) - far_outs),
            out_shape=shapes,
            scratch_shapes=room
            + [pltpu.VMEM(shape, kind) for shape, kind in scratch]
            + ([pltpu.SemaphoreType.DMA((sems,))] if sems else []),
            compiler_params=pltpu.CompilerParams(vmem_limit_bytes=limit * 1024 * 1024),
            cost_estimate=cost(micros),
            name=name,
        )(*far, *near, *wait_for)

    low_rows, full_rows = ((tokens, width), BF16), ((tokens, two), F32)
    lane_rows = ((lanes, seg, width), BF16)
    xs, normed, loc, pair, powers, keep = call(
        functools.partial(first_kernel, short), "forward_local", 4,
        [
            low_rows, low_rows, full_rows, ((2 * lanes, two), F32), ((span, two), F32),
            ((lanes * CHUNKS, two), F32),
        ],
        [bucket_id[0], assignment, block_in[0], gain, b_proj, gamma, nu, theta], [],
        scratch=[low_rows, low_rows, full_rows], sems=4 * lanes + 7, far_outs=3, limit=12,
    )
    enter, cotangent_later = entering(pair, False, cotangent[0])
    (cts,) = call(
        order_kernel, "cotangent_order", 2, [low_rows], [cotangent_later], [],
        scratch=[low_rows], sems=2 * lanes, far_outs=1, limit=8,
    )

    chunk_rows, half_rows = ((lanes * CHUNKS, two), F32), ((n, width), F32)
    out, h, grad_mixed, adj, carry, back_total, grad_d, w_send, states, gelu, pre, low = call(
        block_kernel, "block", 10,
        [
            low_rows, full_rows, full_rows, full_rows, chunk_rows, ((lanes, two), F32), ((1, width), F32),
            ((n, 2 * width), F32), low_rows, low_rows, ((tokens, 2 * width), BF16), low_rows,
        ],
        [glu_weight, c_proj, skip, xs, normed, loc, cts], [enter, powers, keep], fetched=(),
        scratch=[
            chunk_rows, ((width, 2 * width), BF16), ((two, width), BF16), ((1, width), F32),
            low_rows, low_rows, full_rows, low_rows, low_rows, full_rows, full_rows, full_rows,
        ],
        sems=4 * lanes + 12, far_outs=5, limit=30,
    )
    c_keep, w_keep, c_send = call(
        own_kernel, "own_grads", 2, [half_rows, ((n, 2 * width), F32), half_rows],
        [], [gelu, pre, states, low], scratch=[half_rows], sems=1, far_outs=1, limit=8,
    )

    decay = pair[lanes:]
    back_pair = jnp.concatenate(
        [back_total, jnp.concatenate([decay[:, :n], -decay[:, n:]], 1)], 0
    )
    near, last = len(bits("dp")), len(phases()[0]) - 1
    c_got = swap(c_send, "seq", 0)

    def split(keep, got, phase):
        half = ((keep.shape[0] // 2, keep.shape[1]), F32)
        return call(
            functools.partial(split_kernel, phase), "split_sum", 0.5, [half, half], [], [keep, got], pin=True
        )

    own, send = split(w_keep, swap(w_send, "seq", 0), -1)
    leave, own = entering(back_pair, True, own)
    owns = [own]
    for phase in range(1, last):
        own, send = split(own, hop(send, -phase), -1 - phase)
        owns.append(own)
    w = (own + hop(send, -last))[None]
    w_steps = [functools.partial(double, phase=-1 - last)]
    w_steps += [only(functools.partial(gather, phase=-1 - p)) for p in reversed(range(last))]
    for step in w_steps:
        w, _ = step(w)

    back_low, b_keep, b_send, c = call(
        states_kernel, "adjoint_states", 3,
        [low_rows, ((n + 8, two), F32), ((n + 8, two), F32), half_rows],
        [c_keep, h, adj, normed], [carry, b_proj, gamma, skip, leave, powers, keep, grad_d, c_got], fetched=(),
        scratch=[full_rows, full_rows, low_rows, low_rows, ((CHUNKS, two), F32), ((16, two), F32)],
        sems=3 * lanes + 2, far_outs=1, limit=14, wait_for=[owns[1]],
    )

    def back_input(back_low):
        return call(
            input_kernel, "back_input", 4, [lane_rows, lane_rows],
            [gain, b_proj, skip, xs, cts, back_low, grad_mixed, out], [], wait_for=[cb, finished[0], w],
            scratch=[lane_rows, lane_rows], sems=7 * lanes + 3, far_outs=2, limit=12,
        )

    groups = lax.axis_size("dp")
    cut = n // groups
    piece_rows = ((cut, width), F32)
    c_own, *c_sends = call(c_pieces_kernel, "c_pieces", 0.5, [piece_rows] * groups, [], [c])
    c, _ = sum_dp(c_own[None], [v[None] for v in c_sends], None)
    small, b_own, *b_sends = call(
        b_pieces_kernel, "b_pieces", 0.5,
        [((8, two), F32), piece_rows] + [((cut + 8, width), F32)] * (groups - 1),
        [], [b_keep, swap(b_send, "seq", 0)], wait_for=[owns[2]],
    )
    b, small = sum_dp(b_own[None], b_sends, small)
    cb = jnp.concatenate([c, b], 0)

    steps = [functools.partial(scatter, phase=p) for p in range(near, last)]
    steps += [functools.partial(double, phase=last)]
    steps += [only(functools.partial(gather, phase=p)) for p in reversed(range(near, last))]
    for step in steps:
        cb, small = step(cb, extra=small)
    got = swap(small, "seq", 0)
    small = join_rows([small[None], got[None]], lax.axis_index("seq") % 2)[0]
    finished = call(
        finish_kernel, "finish", 1, [((1, v), F32) for v in (width, n, n, n, width)],
        [nu, theta, gain], [small, powers], sems=3,
    )
    grad_in, block_out = back_input(back_low)
    cb, w = tie(cb, w)
    cb = gather_dp(cb)
    cb, grad_in, block_out = tie(cb, grad_in, block_out)
    w, cb = w[0], jnp.concatenate([cb[0], cb[1]], 1)

    grad_gain, grad_gamma, grad_nu, grad_theta, grad_d = finished

    def assemble(mine, widths, wait_for):
        return call(
            assemble_kernel, "assemble", 2, [((2 * mine.shape[0], v), F32) for v in widths],
            [], [mine, swap(mine, "seq", 0)], sems=2 * len(widths), far_outs=len(widths), pin=True, wait_for=wait_for,
        )

    (grad_w,) = assemble(w, [2 * width], [grad_in])
    grad_c, grad_b = assemble(cb, [width, two], [])
    return (
        block_out[None], grad_in[None], grad_gain[0], grad_b, grad_gamma[0], grad_nu[0], grad_theta[0],
        grad_c, grad_d[0], grad_w,
    )


def solution(mesh):
    rows = P("dp", None, "seq", None)
    in_specs = (rows, rows, P("dp", None, None), P("dp", None)) + (P(),) * 8
    out_specs = (rows, rows) + (P(),) * 8
    return jax.shard_map(
        on_device, mesh=mesh, in_specs=in_specs, out_specs=out_specs, check_vma=False
    )
```
